256 devices in a mesh: replica: 16 (over z, core), mp: 16 (over y, x).
Axes of the slice: x: 4, y: 4, z: 8, core: 2. Of those that a mesh axis runs over, the one named last changes fastest.
Arguments:
- pre_act: bfloat16 [2400, 32768], P('mp', 'replica'), may hold values from -6 to 6
- out_grad: bfloat16 [32768, 4800], P(('replica', 'mp')), may hold values from -6 to 6
- weight: bfloat16 [2400, 4800], P('mp'), may hold values from -0.09375 to 0.09375
- error: float32 [16, 2400, 4800], P('replica', 'mp'), may hold values from -96 to 96
- q_init: float32 [4800, 32], replicated, may hold values from -6 to 6
Outputs:
- pre_grad: bfloat16 [2400, 32768], P('mp', 'replica')
- new_error: float32 [16, 2400, 4800], P('replica', 'mp')
- q_new: float32 [4800, 32], replicated
The draws below stay inside these ranges and needn't reach their ends.
All inputs are finite; a program needn't handle non-finite values.
Results may differ from the reference program's by a relative error of at most 0.013.
Values may be sent and summed in bfloat16 or wider, within the bound.
No kernel may reach another device: no remote copies, remote signals or barrier semaphores. Data moves between devices by JAX's collectives and lax.ppermute only.
A program may use at most 128 MiB of HBM per device.

```python
import jax
import jax.numpy as jnp
from jax import lax

D = 4800
HID = 2400
RANK = 32
TOK_GROUP = 2048
TOKENS = 32768
N_REPLICA = 16


def steps_of(rng, extent, split, least, largest):
    factor_of, own = 1.0, jax.random.fold_in(rng, 6)
    for axis_at, shards_of in split:
        heights = jnp.exp(jax.random.uniform(jax.random.fold_in(own, axis_at), (shards_of,), jnp.float32, least / len(split), largest / len(split)))
        factor_of = factor_of * jnp.repeat(heights, extent[axis_at] // shards_of).reshape([-1 if axis == axis_at else 1 for axis in range(len(extent))])
    return factor_of


def normal_values(key, extent, width, bound, shards=(), held_as=jnp.bfloat16):
    drawn = width * jax.random.normal(key, extent, jnp.float32)
    if shards:
        drawn = drawn * steps_of(key, extent, shards, -0.22, 0.18)
    return jnp.clip(drawn, -bound, bound).astype(held_as)


def setup_inputs(seed: int = 0) -> dict:
    keys = jax.random.split(jax.random.key(seed), 6)
    return {
        "pre_act": normal_values(keys[0], (HID, TOKENS), 1.0, 6.0, ((0, 16), (1, 16))),
        "out_grad": normal_values(keys[1], (TOKENS, D), 1.0, 6.0, ((0, 256),)),
        "weight": normal_values(keys[2], (HID, D), D ** -0.5, 0.09375, ((0, 16),)),
        "error": normal_values(keys[3], (N_REPLICA, HID, D), 16.0, 96.0, ((0, 16), (1, 16)), jnp.float32),
        "q_init": normal_values(keys[4], (D, RANK), 1.0, 6.0, (), jnp.float32),
    }


def gelu_back(pre, grad):
    _, pull = jax.vjp(jax.nn.gelu, pre)
    return pull(grad)[0]

def reference(pre_act, out_grad, weight, error, q_init):
    hi = lax.Precision.HIGHEST
    act = jax.nn.gelu(pre_act.astype(jnp.float32)).astype(jnp.bfloat16)
    pieces = []
    mats = []
    psum_total = jnp.zeros((HID, RANK), jnp.float32)
    for group in range(N_REPLICA):
        lo = group * TOK_GROUP
        rows = out_grad[lo:lo + TOK_GROUP]
        back = jnp.dot(weight.astype(jnp.float32), rows.T.astype(jnp.float32), preferred_element_type=jnp.float32)
        pieces.append(gelu_back(pre_act[:, lo:lo + TOK_GROUP].astype(jnp.float32), back).astype(jnp.bfloat16))
        grad = jnp.dot(act[:, lo:lo + TOK_GROUP].astype(jnp.float32), rows.astype(jnp.float32), preferred_element_type=jnp.float32)
        mat = grad + error[group]
        mats.append(mat)
        psum_total = psum_total + jnp.dot(mat, q_init, precision=hi)
    pbar = psum_total / N_REPLICA
    gram = jnp.dot(pbar.T, pbar, precision=hi)
    lower = jnp.linalg.cholesky(gram)
    phat = jax.scipy.linalg.solve_triangular(lower, pbar.T, lower=True).T
    q_total = jnp.zeros((D, RANK), jnp.float32)
    for group in range(N_REPLICA):
        q_total = q_total + jnp.dot(mats[group].T, phat, precision=hi)
    q_new = q_total / N_REPLICA
    approx = jnp.dot(phat, q_new.T, precision=hi)
    new_error = jnp.stack([mat - approx for mat in mats])
    return (jnp.concatenate(pieces, axis=1), new_error, q_new)
```

```python
import jax
import jax.numpy as jnp
from jax import lax
from jax.sharding import PartitionSpec as P

F32 = jnp.float32
BF16 = jnp.bfloat16


def gelu_back(pre, grad):
    _, pull = jax.vjp(jax.nn.gelu, pre)
    return pull(grad)[0]


def gelu16(pre):
    return jax.nn.gelu(pre.astype(F32)).astype(BF16)


def split(x, parts):
    out = []
    for _ in range(parts):
        top = lax.reduce_precision(x, 8, 7)
        out.append(top.astype(BF16))
        x = x - top
    return out


def dot(a, b, ca, cb):
    return lax.dot_general(a, b, (((ca,), (cb,)), ((), ())), preferred_element_type=F32)


def fold(x, parts, axis=0):
    n = x.shape[axis] // parts
    return sum(lax.slice_in_dim(x, i * n, (i + 1) * n, axis=axis) for i in range(parts))


def spread(x, axis):
    n = lax.axis_size(axis)
    return lax.all_to_all(jnp.broadcast_to(x, (n,) + x.shape), axis, 0, 0, tiled=True)


def shards(pre_act, out_grad, weight, error, q_init):
    hi = lax.Precision.HIGHEST
    groups = lax.axis_size("replica")
    mp = lax.axis_size("mp")
    rank = q_init.shape[1]
    hid, toks = pre_act.shape
    own, feat = out_grad.shape
    error = error[0]

    cut = feat // 256 * 128
    blocks = [(0, cut), (cut, feat)]
    pieces = [lax.all_gather(out_grad[:, lo:up], "mp", axis=0, tiled=True) for lo, up in blocks]

    q3 = jnp.concatenate(split(q_init, 3), axis=1)
    y = fold(dot(q3, out_grad, 0, 1), 3)
    y3 = jnp.concatenate(split(y, 3), axis=0)
    mine = pre_act.reshape(hid, mp, own).transpose(1, 0, 2)
    room = -(-hid // 16) * 16
    sent = jnp.concatenate(
        [mine, jnp.zeros((mp, room - hid, own), BF16), jnp.broadcast_to(y3, (mp,) + y3.shape)], axis=1
    )
    got = lax.all_to_all(sent, "mp", 0, 0, tiled=True)
    act_own = gelu16(got[:, :hid])
    y_all = got[:, room:].transpose(1, 0, 2).reshape(3 * rank, toks)
    act = gelu16(pre_act)
    e2 = split(error, 2)
    p_err = sum(fold(dot(q3, e, 0, 1), 3) for e in e2)
    p_local = fold(dot(y_all, act, 1, 1), 3) + p_err
    pbar = jnp.sum(spread(p_local, "replica"), axis=0) / groups
    p_all = spread(pbar, "mp")

    gram = jnp.einsum("mih,mjh->ij", p_all, p_all, precision=hi)
    lower = jnp.linalg.cholesky(gram)
    inv = jax.scipy.linalg.solve_triangular(lower, jnp.eye(rank, dtype=F32), lower=True)

    p3 = jnp.concatenate(split(p_all, 3), axis=1)
    z = fold(lax.dot_general(p3, act_own, (((2,), (1,)), ((0,), (0,))), preferred_element_type=F32).sum(0), 3)
    z3 = jnp.concatenate(split(z, 3), axis=0)
    l3 = jnp.concatenate(split(pbar, 3), axis=0)
    r_local = fold(dot(z3, out_grad, 1, 0), 3) + sum(fold(dot(l3, e, 1, 0), 3) for e in e2)
    rows = r_local.reshape(mp, rank // mp, feat)
    r_part = jnp.sum(lax.all_to_all(rows, "mp", 0, 0, tiled=True), axis=0)
    r_part = jnp.sum(spread(r_part, "replica"), axis=0) / groups
    r_all = spread(r_part, "mp").reshape(rank, feat)
    q_t = jnp.dot(inv, r_all, precision=hi)
    phat = jnp.dot(inv, pbar, precision=hi)

    ph, pl = split(phat, 2)
    qh, ql = split(q_t, 2)
    left = jnp.concatenate([ph, ph, pl], axis=0)
    right = jnp.concatenate([qh, ql, qh], axis=0)
    back = 0.0
    errs = []
    for (lo, up), piece in zip(blocks, pieces):
        back = back + dot(weight[:, lo:up], piece, 1, 1)
        mat = dot(act, piece, 1, 0) + error[:, lo:up]
        errs.append(mat - dot(left, right[:, lo:up], 0, 0))
    pre_grad = gelu_back(pre_act.astype(F32), back).astype(BF16)
    new_error = jnp.concatenate(errs, axis=1)[None]
    return (pre_grad, new_error, q_t.T)


def solution(mesh):
    return jax.shard_map(
        shards,
        mesh=mesh,
        in_specs=(
            P("mp", "replica"),
            P(("replica", "mp"), None),
            P("mp", None),
            P("replica", "mp", None),
            P(),
        ),
        out_specs=(P("mp", "replica"), P("replica", "mp", None), P()),
        check_vma=False,
    )
```

```python
import jax
import jax.numpy as jnp
import numpy as np
from jax import lax
from jax.experimental import pallas as pl
from jax.experimental.pallas import tpu as pltpu
from jax.sharding import Mesh, PartitionSpec as P

F32 = jnp.float32
BF16 = jnp.bfloat16
MP = ("y", "x")
ALL = ("z", "core", "y", "x")


def gelu_back(pre, grad):
    _, pull = jax.vjp(jax.nn.gelu, pre)
    return pull(grad)[0]


def gelu16(pre):
    return jax.nn.gelu(pre.astype(F32)).astype(BF16)


def split(x, parts):
    out = []
    for _ in range(parts):
        top = lax.reduce_precision(x, 8, 7)
        out.append(top.astype(BF16))
        x = x - top
    return out


def dot(a, b, ca, cb):
    return lax.dot_general(a, b, (((ca,), (cb,)), ((), ())), preferred_element_type=F32)


def fold(x, parts, axis=0):
    n = x.shape[axis] // parts
    return sum(lax.slice_in_dim(x, i * n, (i + 1) * n, axis=axis) for i in range(parts))


def spread(x, axis):
    n = lax.axis_size(axis)
    return lax.all_to_all(jnp.broadcast_to(x, (n,) + x.shape), axis, 0, 0, tiled=True)


def other_core(x):
    return lax.ppermute(x, "core", [(0, 1), (1, 0)])


def shift(x, sizes, along_b, step):
    nz, nc, ny, nx = sizes
    at = lambda z, c, y, w: ((z * nc + c) * ny + y % ny) * nx + w % nx
    perm = []
    for z, c, y, w in np.ndindex(*sizes):
        along_x = along_b == (c == 0)
        src = at(z, c, y, w + step) if along_x else at(z, c, y + step, w)
        perm.append((src, at(z, c, y, w)))
    return lax.ppermute(x, ALL, perm)


def products(where, pre_ref, weight_ref, b0, b1, b2, b3, mat_in, grad_in, mat_ref, grad_ref):
    grad_ref[...] = grad_in[...]
    own = b0.shape[1]
    blocks = (b0, b1, b2, b3)
    spots = [pl.ds(pl.multiple_of(where[i] * own, own), own) for i in range(4)]
    pre = jnp.concatenate([pre_ref[:, s] for s in spots], axis=1).astype(F32)
    act, pull = jax.vjp(jax.nn.gelu, pre)
    act = act.astype(BF16)
    feat = weight_ref.shape[1]
    back = jnp.zeros(pre.shape, F32)
    for lo in range(0, feat, 512):
        part = slice(lo, min(feat, lo + 512))
        piece = jnp.concatenate([b[part, :] for b in blocks], axis=1)
        back = back + dot(weight_ref[:, part], piece, 1, 0)
        mat_ref[:, part] = mat_in[:, part] + dot(act, piece, 1, 1)
    out = pull(back)[0].astype(BF16)
    for i, s in enumerate(spots):
        grad_ref[:, s] = out[:, i * own:(i + 1) * own]


def add_products(where, pre_act, weight, blocks, mat, pre_grad):
    vmem = pl.BlockSpec(memory_space=pltpu.VMEM)
    return pl.pallas_call(
        products,
        out_shape=(jax.ShapeDtypeStruct(mat.shape, F32), jax.ShapeDtypeStruct(pre_grad.shape, BF16)),
        in_specs=[pl.BlockSpec(memory_space=pltpu.SMEM)] + [vmem] * 8,
        out_specs=(vmem, vmem),
        input_output_aliases={7: 0, 8: 1},
        compiler_params=pltpu.CompilerParams(vmem_limit_bytes=40 * 2**20),
    )(where, pre_act, weight, *blocks, mat, pre_grad)


def shards(sizes, pre_act, out_grad, weight, error, q_init):
    hi = lax.Precision.HIGHEST
    nz, nc, ny, nx = sizes
    groups = nz * nc
    mp = ny * nx
    rank = q_init.shape[1]
    half = rank // 2
    hid, toks = pre_act.shape
    own, feat = out_grad.shape
    error = error[0]
    core = lax.axis_index("core")

    got = {(0, 0): out_grad.T}
    along_a = lambda k, step: shift(got[k], sizes, False, step)
    along_b = lambda k, step: shift(got[k], sizes, True, step)

    def tie(value, keys):
        out = lax.optimization_barrier([value] + [got[k] for k in keys])
        got.update(zip(keys, out[1:]))
        return out[0]

    for step in (1, -1):
        got[0, step] = along_b((0, 0), step)
        got[step, 0] = along_a((0, 0), step)

    act = gelu16(pre_act)
    q3 = jnp.concatenate(split(q_init, 3), axis=1)
    y = fold(dot(q3, out_grad, 0, 1), 3)
    y_all = spread(y, MP).transpose(1, 0, 2).reshape(rank, toks)
    y3 = jnp.concatenate(split(y_all, 3), axis=0)
    e2 = split(error, 2)
    p_err = sum(fold(dot(q3, e, 0, 1), 3) for e in e2)
    p_local = fold(dot(y3, act, 1, 1), 3) + p_err
    p_local = tie(p_local, [(0, 1), (0, -1), (1, 0), (-1, 0)])
    got[0, 2] = along_b((0, 1), 1)
    got[2, 0] = along_a((1, 0), 1)
    for db in (1, -1):
        for da in (1, -1):
            got[da, db] = along_a((0, db), da)
    pbar = jnp.sum(spread(p_local, "z"), axis=0)
    pbar = (pbar + other_core(pbar)) / groups

    l3 = jnp.concatenate(split(pbar, 3), axis=0)
    z_part = fold(dot(l3, act, 1, 0), 3)
    gram_part = jnp.dot(pbar, pbar.T, precision=hi)
    side = 128 // rank
    flat = jnp.concatenate(jnp.split(gram_part, side, axis=0), axis=1)
    sent = jnp.concatenate(
        [
            z_part.reshape(rank, mp, own).transpose(1, 0, 2),
            jnp.broadcast_to(flat, (mp,) + flat.shape),
        ],
        axis=1,
    )
    took = jnp.sum(lax.all_to_all(sent, MP, 0, 0, tiled=True), axis=0)
    z = took[:rank]
    gram = jnp.concatenate(jnp.split(took[rank:], side, axis=1), axis=0)

    z3 = jnp.concatenate(split(z, 3), axis=0)
    r_local = fold(dot(z3, out_grad, 1, 0), 3) + sum(fold(dot(l3, e, 1, 0), 3) for e in e2)
    low, high = r_local[:half], r_local[half:]
    keep = jnp.where(core == 0, low, high) + other_core(jnp.where(core == 0, high, low))
    r_part = lax.all_to_all(keep.reshape(mp, half // mp, feat), MP, 0, 0, tiled=True)
    r_part = jnp.sum(r_part, axis=0)
    r_part = tie(r_part, [(0, 2), (2, 0), (1, 1), (-1, 1), (1, -1), (-1, -1)])
    got[1, 2] = along_a((0, 2), 1)
    got[-1, 2] = along_a((0, 2), -1)
    got[2, 1] = along_a((1, 1), 1)
    got[2, -1] = along_a((-1, -1), -1)
    r_part = jnp.sum(spread(r_part, "z"), axis=0) / groups
    mine = spread(r_part, MP).reshape(half, feat)
    mine = tie(mine, [(1, 2)])
    got[2, 2] = along_a((1, 2), 1)
    theirs = other_core(mine)
    r_all = jnp.concatenate([jnp.where(core == 0, mine, theirs), jnp.where(core == 0, theirs, mine)], axis=0)

    lower = jnp.linalg.cholesky(gram)
    inv = jax.scipy.linalg.solve_triangular(lower, jnp.eye(rank, dtype=F32), lower=True)
    q_t = jnp.dot(inv, r_all, precision=hi)
    phat = jnp.dot(inv, pbar, precision=hi)

    iy, ix = lax.axis_index("y"), lax.axis_index("x")
    ia, ib = jnp.where(core == 0, iy, ix), jnp.where(core == 0, ix, iy)
    mat, pre_grad = error, jnp.zeros_like(pre_act)
    for da in (0, 1, -1, 2):
        keys = [(da, db) for db in (0, 1, -1, 2)]
        a, b = (ia + da) & 3, (ib + jnp.array([0, 1, -1, 2])) & 3
        where = jnp.where(core == 0, a * nx + b, b * nx + a)
        mat, pre_grad = add_products(where, pre_act, weight, [got[k] for k in keys], mat, pre_grad)

    ph, pw = split(phat, 2)
    qh, ql = split(q_t, 2)
    left = jnp.concatenate([ph, ph, pw], axis=0)
    right = jnp.concatenate([qh, ql, qh], axis=0)
    new_error = (mat - dot(left, right, 0, 0))[None]
    return (pre_grad, new_error, q_t.T)


def solution(mesh):
    sizes = (mesh.shape["replica"] // 2, 2, 4, mesh.shape["mp"] // 4)
    grid = Mesh(mesh.devices.reshape(sizes), ALL)

    def run(*args):
        return shards(sizes, *args)

    return jax.shard_map(
        run,
        mesh=grid,
        in_specs=(
            P(MP, ("z", "core")),
            P(ALL, None),
            P(MP, None),
            P(("z", "core"), MP, None),
            P(),
        ),
        out_specs=(P(MP, ("z", "core")), P(("z", "core"), MP, None), P()),
        check_vma=False,
    )
```

```python
import jax
import jax.numpy as jnp
import numpy as np
from jax import lax
from jax.experimental import pallas as pl
from jax.experimental.pallas import tpu as pltpu
from jax.sharding import Mesh, PartitionSpec as P

F32 = jnp.float32
BF16 = jnp.bfloat16
MP = ("y", "x")
ALL = ("z", "core", "y", "x")


def gelu_back(pre, grad):
    _, pull = jax.vjp(jax.nn.gelu, pre)
    return pull(grad)[0]


def gelu16(pre):
    return jax.nn.gelu(pre.astype(F32)).astype(BF16)


def split(x, parts):
    out = []
    for _ in range(parts):
        top = lax.reduce_precision(x, 8, 7)
        out.append(top.astype(BF16))
        x = x - top
    return out


def dot(a, b, ca, cb):
    return lax.dot_general(a, b, (((ca,), (cb,)), ((), ())), preferred_element_type=F32)


def fold(x, parts, axis=0):
    n = x.shape[axis] // parts
    return sum(lax.slice_in_dim(x, i * n, (i + 1) * n, axis=axis) for i in range(parts))


def spread(x, axis):
    n = lax.axis_size(axis)
    return lax.all_to_all(jnp.broadcast_to(x, (n,) + x.shape), axis, 0, 0, tiled=True)


def other_core(x):
    return lax.ppermute(x, "core", [(0, 1), (1, 0)])


def shift(x, axis, step):
    n = lax.axis_size(axis)
    return lax.ppermute(x, axis, [((i + step) % n, i) for i in range(n)])


def products(where, pre_ref, weight_ref, *refs):
    *blocks, mat_in, grad_in, mat_ref, grad_ref = refs
    grad_ref[...] = grad_in[...]
    own = blocks[0].shape[1]
    spots = [pl.ds(pl.multiple_of(where[i] * own, own), own) for i in range(len(blocks))]
    pre = jnp.concatenate([pre_ref[:, s] for s in spots], axis=1).astype(F32)
    act, pull = jax.vjp(jax.nn.gelu, pre)
    act = act.astype(BF16)
    feat = weight_ref.shape[1]
    back = jnp.zeros(pre.shape, F32)
    for lo in range(0, feat, 512):
        part = slice(lo, min(feat, lo + 512))
        piece = jnp.concatenate([b[part, :] for b in blocks], axis=1)
        back = back + dot(weight_ref[:, part], piece, 1, 0)
        mat_ref[:, part] = mat_in[:, part] + dot(act, piece, 1, 1)
    out = pull(back)[0].astype(BF16)
    for i, s in enumerate(spots):
        grad_ref[:, s] = out[:, i * own:(i + 1) * own]


def add_products(where, pre_act, weight, blocks, mat, pre_grad):
    vmem = pl.BlockSpec(memory_space=pltpu.VMEM)
    n = len(blocks)
    return pl.pallas_call(
        products,
        out_shape=(jax.ShapeDtypeStruct(mat.shape, F32), jax.ShapeDtypeStruct(pre_grad.shape, BF16)),
        in_specs=[pl.BlockSpec(memory_space=pltpu.SMEM)] + [vmem] * (n + 4),
        out_specs=(vmem, vmem),
        input_output_aliases={n + 3: 0, n + 4: 1},
        compiler_params=pltpu.CompilerParams(vmem_limit_bytes=40 * 2**20),
    )(where, pre_act, weight, *blocks, mat, pre_grad)


def shards(sizes, pre_act, out_grad, weight, error, q_init):
    hi = lax.Precision.HIGHEST
    nz, nc, ny, nx = sizes
    groups = nz * nc
    mp = ny * nx
    rank = q_init.shape[1]
    half = rank // 2
    hid, toks = pre_act.shape
    own, feat = out_grad.shape
    error = error[0]
    core = lax.axis_index("core")

    got = {(0, 0): out_grad.T}
    iy, ix = lax.axis_index("y"), lax.axis_index("x")
    state = [error, jnp.zeros_like(pre_act)]

    def fetch(*moves):
        new = {}
        for key, axis, step in moves:
            dy, dx = (key[0] + step, key[1]) if axis == "y" else (key[0], key[1] + step)
            new[dy % ny, dx % nx] = shift(got[key[0] % ny, key[1] % nx], axis, step)
        got.update(new)
        return list(new)

    def tie(value, keys=(), with_state=False):
        out = lax.optimization_barrier([value, [got[k] for k in keys], state if with_state else []])
        got.update(zip(keys, out[1]))
        if with_state:
            state[:] = out[2]
        return out[0]

    def use(keys):
        where = jnp.stack([((iy + dy) & (ny - 1)) * nx + ((ix + dx) & (nx - 1)) for dy, dx in keys])
        state[:] = add_products(where, pre_act, weight, [got[k] for k in keys], *state)

    act = gelu16(pre_act)
    q3 = jnp.concatenate(split(q_init, 3), axis=1)
    y = fold(dot(q3, out_grad, 0, 1), 3)
    y_all = tie(spread(y, MP), [(0, 0)])
    one = fetch(((0, 0), "x", 1), ((0, 0), "x", -1), ((0, 0), "y", 1), ((0, 0), "y", -1))
    y_all = y_all.transpose(1, 0, 2).reshape(rank, toks)
    y3 = jnp.concatenate(split(y_all, 3), axis=0)
    e2 = split(error, 2)
    p_err = sum(fold(dot(q3, e, 0, 1), 3) for e in e2)
    p_local = fold(dot(y3, act, 1, 1), 3) + p_err
    pbar = jnp.sum(spread(p_local, "z"), axis=0)
    pbar = tie((pbar + other_core(pbar)) / groups, one)

    l3 = jnp.concatenate(split(pbar, 3), axis=0)
    z_part = fold(dot(l3, act, 1, 0), 3)
    gram_part = jnp.dot(pbar, pbar.T, precision=hi)
    side = 128 // rank
    flat = jnp.concatenate(jnp.split(gram_part, side, axis=0), axis=1)
    sent = jnp.concatenate(
        [
            z_part.reshape(rank, mp, own).transpose(1, 0, 2),
            jnp.broadcast_to(flat, (mp,) + flat.shape),
        ],
        axis=1,
    )
    took = tie(lax.all_to_all(sent, MP, 0, 0, tiled=True), one)
    two = fetch(((0, 1), "y", 1), ((0, -1), "y", -1), ((1, 0), "x", -1), ((-1, 0), "x", 1))
    use([(0, 0)] + one)
    took = jnp.sum(took, axis=0)
    z = took[:rank]
    gram = jnp.concatenate(jnp.split(took[rank:], side, axis=1), axis=0)

    z3 = jnp.concatenate(split(z, 3), axis=0)
    r_local = fold(dot(z3, out_grad, 1, 0), 3) + sum(fold(dot(l3, e, 1, 0), 3) for e in e2)
    low, high = r_local[:half], r_local[half:]
    keep = jnp.where(core == 0, low, high) + other_core(jnp.where(core == 0, high, low))
    r_part = lax.all_to_all(keep.reshape(nz, half // nz, feat), "z", 0, 0, tiled=True)
    r_part = tie(jnp.sum(r_part, axis=0), two, True)
    r_part = tie(spread(r_part, MP), two)
    three = fetch(((0, 1), "x", 1), ((1, 0), "y", 1), ((1, -1), "x", -1), ((-1, 1), "y", -1))
    use(two)
    r_part = jnp.sum(r_part, axis=0) / groups
    mine = tie(spread(r_part, "z"), three, True).reshape(half, feat)
    four = fetch(((-1, 1), "x", 1), ((1, 2), "y", 1), ((-1, -1), "y", -1))
    use(three)
    use(four)
    theirs = other_core(mine)
    r_all = jnp.concatenate([jnp.where(core == 0, mine, theirs), jnp.where(core == 0, theirs, mine)], axis=0)

    lower = jnp.linalg.cholesky(gram)
    inv = jax.scipy.linalg.solve_triangular(lower, jnp.eye(rank, dtype=F32), lower=True)
    q_t = jnp.dot(inv, r_all, precision=hi)
    phat = jnp.dot(inv, pbar, precision=hi)

    mat, pre_grad = state
    ph, pw = split(phat, 2)
    qh, ql = split(q_t, 2)
    left = jnp.concatenate([ph, ph, pw], axis=0)
    right = jnp.concatenate([qh, ql, qh], axis=0)
    new_error = (mat - dot(left, right, 0, 0))[None]
    return (pre_grad, new_error, q_t.T)


def solution(mesh):
    sizes = (mesh.shape["replica"] // 2, 2, 4, mesh.shape["mp"] // 4)
    grid = Mesh(mesh.devices.reshape(sizes), ALL)

    def run(*args):
        return shards(sizes, *args)

    return jax.shard_map(
        run,
        mesh=grid,
        in_specs=(
            P(MP, ("z", "core")),
            P(ALL, None),
            P(MP, None),
            P(("z", "core"), MP, None),
            P(),
        ),
        out_specs=(P(MP, ("z", "core")), P(("z", "core"), MP, None), P()),
        check_vma=False,
    )
```

```python
import functools

import jax
import jax.numpy as jnp
from jax import lax
from jax.experimental import pallas as pl
from jax.experimental.pallas import tpu as pltpu
from jax.sharding import Mesh, PartitionSpec as P

F32 = jnp.float32
BF16 = jnp.bfloat16
MP = ("y", "x")
ALL = ("z", "core", "y", "x")


def gelu_back(pre, grad):
    _, pull = jax.vjp(jax.nn.gelu, pre)
    return pull(grad)[0]


def gelu16(pre):
    return jax.nn.gelu(pre.astype(F32)).astype(BF16)


def split(x, parts):
    out = []
    for _ in range(parts):
        top = lax.reduce_precision(x, 8, 7)
        out.append(top.astype(BF16))
        x = x - top
    return out


def dot(a, b, ca, cb):
    return lax.dot_general(a, b, (((ca,), (cb,)), ((), ())), preferred_element_type=F32)


def fold(x, parts, axis=0):
    n = x.shape[axis] // parts
    return sum(lax.slice_in_dim(x, i * n, (i + 1) * n, axis=axis) for i in range(parts))


def spread(x, axis):
    n = lax.axis_size(axis)
    return lax.all_to_all(jnp.broadcast_to(x, (n,) + x.shape), axis, 0, 0, tiled=True)


def other_core(x):
    return lax.ppermute(x, "core", [(0, 1), (1, 0)])


def shift(x, axis, step):
    n = lax.axis_size(axis)
    return lax.ppermute(x, axis, [((i + step) % n, i) for i in range(n)])


def partner(x):
    return lax.ppermute(x, "x", [(i, i ^ 1) for i in range(lax.axis_size("x"))])


def peer(x):
    n = lax.axis_size("x")
    return lax.ppermute(x, "x", [(i, n - 1 - i) for i in range(n)])


def products(n, first, last, where, pre_a, pre_b, w_a, w_b, *refs):
    refs = list(refs)
    blocks = [[refs.pop(0) for _ in range(k)] for k in n]
    total = None if first else refs.pop(0)
    keep_ref, send_ref, *outs = refs
    own = blocks[0][0].shape[1]
    rows, feat = w_a.shape
    spots = [pl.ds(pl.multiple_of(where[i] * own, own), own) for i in range(len(blocks))]
    pre = [jnp.concatenate([p[:, s] for s in spots], axis=1) for p in (pre_a, pre_b)]
    act = gelu16(jnp.concatenate(pre, axis=0))
    back = jnp.zeros(act.shape, F32)
    edges, at = [], 0
    for ref in blocks[0]:
        edges.append(at)
        at += ref.shape[0]
    for k, edge in enumerate(edges):
        size = blocks[0][k].shape[0]
        for lo in range(0, size, 512):
            here = slice(lo, min(size, lo + 512))
            part = slice(edge + here.start, edge + here.stop)
            piece = jnp.concatenate([b[k][here, :] for b in blocks], axis=1)
            left = jnp.concatenate([w_a[:, part], w_b[:, part]], axis=0)
            back = back + dot(left, piece, 1, 0)
            more = dot(act, piece, 1, 1)
            if total is not None:
                more = more + total[:, part]
            if last:
                outs[0][:, part] = more[:rows]
                outs[1][:, part] = more[rows:].astype(BF16)
            else:
                outs[0][:, part] = more
    keep_ref[...] = back[:rows]
    send_ref[...] = back[rows:].astype(BF16)


def add_products(where, pre, weight, blocks, total, last=False):
    vmem = pl.BlockSpec(memory_space=pltpu.VMEM)
    rows, feat = weight[0].shape
    toks = sum(b[0].shape[1] for b in blocks)
    flat = [x for b in blocks for x in b] + ([] if total is None else [total])
    shape = jax.ShapeDtypeStruct
    out = [shape((rows, toks), F32), shape((rows, toks), BF16)]
    if last:
        out += [shape((rows, feat), F32), shape((rows, feat), BF16)]
    else:
        out += [shape((2 * rows, feat), F32)]
    return pl.pallas_call(
        functools.partial(products, [len(b) for b in blocks], total is None, last),
        out_shape=out,
        in_specs=[pl.BlockSpec(memory_space=pltpu.SMEM)] + [vmem] * (4 + len(flat)),
        out_specs=[vmem] * len(out),
        compiler_params=pltpu.CompilerParams(vmem_limit_bytes=40 * 2**20),
    )(where, *pre, *weight, *flat)


def grads(counts, own, where, pre_ref, *refs):
    *halves, out_ref = refs
    k = 0
    for n, keep, came in zip(counts, halves[::2], halves[1::2]):
        for i in range(n):
            s = pl.ds(pl.multiple_of(where[k] * own, own), own)
            back = keep[:, i * own:(i + 1) * own] + came[:, i * own:(i + 1) * own].astype(F32)
            out = gelu_back(pre_ref[:, s].astype(F32), back).astype(BF16)
            out_ref[:, s] = out[:out_ref.shape[0]]
            k += 1


def pre_grads(where, pre, rows, own, halves):
    vmem = pl.BlockSpec(memory_space=pltpu.VMEM)
    counts = [a.shape[1] // own for a, _ in halves]
    return pl.pallas_call(
        functools.partial(grads, counts, own),
        out_shape=jax.ShapeDtypeStruct((rows, pre.shape[1]), BF16),
        in_specs=[pl.BlockSpec(memory_space=pltpu.SMEM)] + [vmem] * (1 + 2 * len(halves)),
        out_specs=vmem,
        compiler_params=pltpu.CompilerParams(vmem_limit_bytes=40 * 2**20),
    )(where, pre, *[x for pair in halves for x in pair])


def finish(side, own_ref, came_ref, error_ref, left_ref, right_ref, out_ref):
    rows, feat = error_ref.shape
    width = own_ref.shape[1]
    start = feat - width
    first = side[0] == 0
    left = left_ref[...]
    for base, top, turn in ((0, start, True), (start, feat, False)):
        for lo in range(base, top, 512):
            part = slice(lo, min(top, lo + 512))
            at = slice(part.start - base, part.stop - base)
            mine, came = own_ref[:, at], came_ref[:, at].astype(F32)
            grad = jnp.where(first, mine, came) if turn else jnp.where(first, came, mine)
            out_ref[:, part] = grad[:rows] + error_ref[:, part] - dot(left, right_ref[:, part], 1, 0)


def new_errors(side, own, came, error, left, right):
    vmem = pl.BlockSpec(memory_space=pltpu.VMEM)
    return pl.pallas_call(
        finish,
        out_shape=jax.ShapeDtypeStruct(error.shape, F32),
        in_specs=[pl.BlockSpec(memory_space=pltpu.SMEM)] + [vmem] * 5,
        out_specs=vmem,
        compiler_params=pltpu.CompilerParams(vmem_limit_bytes=40 * 2**20),
    )(side, own, came, error, left, right)


def tie(*values):
    return lax.optimization_barrier(values)


def shards(sizes, pre_act, out_grad, weight, error, q_init):
    hi = lax.Precision.HIGHEST
    nz, nc, ny, nx = sizes
    groups = nz * nc
    mp = ny * nx
    rank = q_init.shape[1]
    half = rank // 2
    hid, toks = pre_act.shape
    own, feat = out_grad.shape
    error = error[0]
    core = lax.axis_index("core")

    iy, ix = lax.axis_index("y"), lax.axis_index("x")

    side = (ix ^ (ix >> 1)) & 1
    start = feat // 256 * 128
    width = feat - start
    rows = -(-hid // 16) * 16
    og = out_grad.T
    og_give = jnp.where(side == 0, og[start:], og[:width])
    og_mine = jnp.where(side == 0, og[:width], og[start:])
    og_came = partner(og_give)
    below = jnp.where((ix & 1) == 0, og_mine, og_came)
    above = jnp.where((ix & 1) == 0, og_came, og_mine)
    block = jnp.concatenate([below, above], axis=1)
    pair = 2 * own
    pre_pad = jnp.pad(pre_act, ((0, rows - hid), (0, 0)))
    w_pad = jnp.pad(weight, ((0, rows - hid), (0, 0)))
    w_first, w_last = w_pad[:, :width], w_pad[:, start:]
    w_last = jnp.where(jnp.arange(width) < width - start, jnp.zeros_like(w_last), w_last)
    w_mine = jnp.where(side == 0, w_first, w_last)
    w_give = jnp.where(side == 0, w_last, w_first)

    def spot(keys):
        return jnp.stack([((iy + dy) & (ny - 1)) * (nx // 2) + ((ix >> 1) ^ j) for j, dy in keys])

    act = gelu16(pre_act)
    q3 = jnp.concatenate(split(q_init, 3), axis=1)
    y = fold(dot(q3, out_grad, 0, 1), 3)
    y_all, block, pre_pad, w_give = tie(spread(y, MP), block, pre_pad, w_give)
    up, down, over = shift(block, "y", 1), shift(block, "y", -1), peer(block)
    pre_two = (pre_pad, partner(pre_pad))
    w_two = (w_mine, partner(w_give))
    y_all = y_all.transpose(1, 0, 2).reshape(rank, toks)
    y3 = jnp.concatenate(split(y_all, 3), axis=0)
    e2 = split(error, 2)
    p_err = sum(fold(dot(q3, e, 0, 1), 3) for e in e2)
    p_local = fold(dot(y3, act, 1, 1), 3) + p_err
    pbar = jnp.sum(spread(p_local, "z"), axis=0)
    pbar, up, down, over = tie((pbar + other_core(pbar)) / groups, up, down, over)

    l3 = jnp.concatenate(split(pbar, 3), axis=0)
    z_part = fold(dot(l3, act, 1, 0), 3)
    gram_part = jnp.dot(pbar, pbar.T, precision=hi)
    quarter = 128 // rank
    flat = jnp.concatenate(jnp.split(gram_part, quarter, axis=0), axis=1)
    sent = jnp.concatenate(
        [
            z_part.reshape(rank, mp, own).transpose(1, 0, 2),
            jnp.broadcast_to(flat, (mp,) + flat.shape),
        ],
        axis=1,
    )
    took, up, down, over = tie(lax.all_to_all(sent, MP, 0, 0, tiled=True), up, down, over)
    far, over_up, over_down = shift(up, "y", 1), peer(up), shift(over, "y", -1)
    keys = [[(0, 0), (0, 1), (0, -1), (1, 0)], [(0, 2), (1, 1), (1, -1)], [(1, 2)]]
    places = [spot(k) for k in keys]
    keep_1, send_1, total = add_products(places[0], pre_two, w_two, [[block], [up], [down], [over]], None)
    took = jnp.sum(took, axis=0)
    z = took[:rank]
    gram = jnp.concatenate(jnp.split(took[rank:], quarter, axis=1), axis=0)

    z3 = jnp.concatenate(split(z, 3), axis=0)
    r_local = fold(dot(z3, out_grad, 1, 0), 3) + sum(fold(dot(l3, e, 1, 0), 3) for e in e2)
    low, high = r_local[:half], r_local[half:]
    keep = jnp.where(core == 0, low, high) + other_core(jnp.where(core == 0, high, low))
    r_part = lax.all_to_all(keep.reshape(nz, half // nz, feat), "z", 0, 0, tiled=True)
    r_part, far, over_up, over_down, total = tie(jnp.sum(r_part, axis=0), far, over_up, over_down, total)
    came_1 = partner(send_1)
    r_part, far, over_up, over_down = tie(spread(r_part, MP), far, over_up, over_down)
    cut = (width // 3 + 64) // 128 * 128
    last = [
        peer(far[:cut]),
        shift(over_up[cut:2 * cut], "y", 1),
        shift(over_down[2 * cut:], "y", -1),
    ]
    keep_2, send_2, total = add_products(places[1], pre_two, w_two, [[far], [over_up], [over_down]], total)
    r_part = jnp.sum(r_part, axis=0) / groups
    mine, total, *last = tie(spread(r_part, "z"), total, *last)
    mine = mine.reshape(half, feat)
    came_2 = partner(send_2)
    keep_3, send_3, grad_mine, grad_give = add_products(places[2], pre_two, w_two, [last], total, True)
    grad_came = partner(grad_give)
    came_3 = partner(send_3)
    halves = [(keep_1, came_1), (keep_2, came_2), (keep_3, came_3)]
    pre_grad = pre_grads(jnp.concatenate(places), pre_pad, hid, pair, halves)
    theirs = other_core(mine)
    r_all = jnp.concatenate([jnp.where(core == 0, mine, theirs), jnp.where(core == 0, theirs, mine)], axis=0)

    lower = jnp.linalg.cholesky(gram)
    inv = jax.scipy.linalg.solve_triangular(lower, jnp.eye(rank, dtype=F32), lower=True)
    q_t = jnp.dot(inv, r_all, precision=hi)
    phat = jnp.dot(inv, pbar, precision=hi)

    ph, pw = split(phat, 2)
    qh, ql = split(q_t, 2)
    left = jnp.concatenate([ph, ph, pw], axis=0).T
    right = jnp.concatenate([qh, ql, qh], axis=0)
    new_error = new_errors(side.reshape(1), grad_mine, grad_came, error, left, right)[None]
    return (pre_grad, new_error, q_t.T)


def solution(mesh):
    sizes = (mesh.shape["replica"] // 2, 2, 4, mesh.shape["mp"] // 4)
    grid = Mesh(mesh.devices.reshape(sizes), ALL)

    def run(*args):
        return shards(sizes, *args)

    return jax.shard_map(
        run,
        mesh=grid,
        in_specs=(
            P(MP, ("z", "core")),
            P(ALL, None),
            P(MP, None),
            P(("z", "core"), MP, None),
            P(),
        ),
        out_specs=(P(MP, ("z", "core")), P(("z", "core"), MP, None), P()),
        check_vma=False,
    )
```

```python
import functools

import jax
import jax.numpy as jnp
from jax import lax
from jax.experimental import pallas as pl
from jax.experimental.pallas import tpu as pltpu
from jax.sharding import Mesh, PartitionSpec as P

F32 = jnp.float32
BF16 = jnp.bfloat16
MP = ("y", "x")
ALL = ("z", "core", "y", "x")


def gelu_back(pre, grad):
    _, pull = jax.vjp(jax.nn.gelu, pre)
    return pull(grad)[0]


def gelu16(pre):
    return jax.nn.gelu(pre.astype(F32)).astype(BF16)


def split(x, parts):
    out = []
    for _ in range(parts):
        top = lax.reduce_precision(x, 8, 7)
        out.append(top.astype(BF16))
        x = x - top
    return out


def dot(a, b, ca, cb):
    return lax.dot_general(a, b, (((ca,), (cb,)), ((), ())), preferred_element_type=F32)


def fold(x, parts, axis=0):
    n = x.shape[axis] // parts
    return sum(lax.slice_in_dim(x, i * n, (i + 1) * n, axis=axis) for i in range(parts))


def spread(x, axis):
    n = lax.axis_size(axis)
    return lax.all_to_all(jnp.broadcast_to(x, (n,) + x.shape), axis, 0, 0, tiled=True)


def other_core(x):
    return lax.ppermute(x, "core", [(0, 1), (1, 0)])


def shift(x, axis, step):
    n = lax.axis_size(axis)
    return lax.ppermute(x, axis, [((i + step) % n, i) for i in range(n)])


def partner(x):
    return lax.ppermute(x, "x", [(i, i ^ 1) for i in range(lax.axis_size("x"))])


def peer(x):
    n = lax.axis_size("x")
    return lax.ppermute(x, "x", [(i, n - 1 - i) for i in range(n)])


def products(n, first, last, where, pre_a, pre_b, w_a, w_b, *refs):
    refs = list(refs)
    blocks = [[refs.pop(0) for _ in range(k)] for k in n]
    total = None if first else refs.pop(0)
    keep_ref, send_ref, *outs = refs
    own = blocks[0][0].shape[1]
    rows, feat = w_a.shape
    spots = [pl.ds(pl.multiple_of(where[i] * own, own), own) for i in range(len(blocks))]
    pre = [jnp.concatenate([p[:, s] for s in spots], axis=1) for p in (pre_a, pre_b)]
    act = gelu16(jnp.concatenate(pre, axis=0))
    back = jnp.zeros(act.shape, F32)
    edges, at = [], 0
    for ref in blocks[0]:
        edges.append(at)
        at += ref.shape[0]
    for k, edge in enumerate(edges):
        size = blocks[0][k].shape[0]
        for lo in range(0, size, 512):
            here = slice(lo, min(size, lo + 512))
            part = slice(edge + here.start, edge + here.stop)
            piece = jnp.concatenate([b[k][here, :] for b in blocks], axis=1)
            left = jnp.concatenate([w_a[:, part], w_b[:, part]], axis=0)
            back = back + dot(left, piece, 1, 0)
            more = dot(act, piece, 1, 1)
            if total is not None:
                more = more + total[:, part]
            if last:
                outs[0][:, part] = more[:rows]
                outs[1][:, part] = more[rows:].astype(BF16)
            else:
                outs[0][:, part] = more
    keep_ref[...] = back[:rows]
    send_ref[...] = back[rows:].astype(BF16)


def add_products(where, pre, weight, blocks, total, last=False):
    vmem = pl.BlockSpec(memory_space=pltpu.VMEM)
    rows, feat = weight[0].shape
    toks = sum(b[0].shape[1] for b in blocks)
    flat = [x for b in blocks for x in b] + ([] if total is None else [total])
    shape = jax.ShapeDtypeStruct
    out = [shape((rows, toks), F32), shape((rows, toks), BF16)]
    if last:
        out += [shape((rows, feat), F32), shape((rows, feat), BF16)]
    else:
        out += [shape((2 * rows, feat), F32)]
    return pl.pallas_call(
        functools.partial(products, [len(b) for b in blocks], total is None, last),
        out_shape=out,
        in_specs=[pl.BlockSpec(memory_space=pltpu.SMEM)] + [vmem] * (4 + len(flat)),
        out_specs=[vmem] * len(out),
        compiler_params=pltpu.CompilerParams(vmem_limit_bytes=40 * 2**20),
    )(where, *pre, *weight, *flat)


def grads(counts, own, where, pre_ref, *refs):
    *halves, out_ref = refs
    k = 0
    for n, keep, came in zip(counts, halves[::2], halves[1::2]):
        for i in range(n):
            s = pl.ds(pl.multiple_of(where[k] * own, own), own)
            j = i ^ 1
            back = keep[:, i * own:(i + 1) * own] + came[:, j * own:(j + 1) * own].astype(F32)
            out = gelu_back(pre_ref[:, s].astype(F32), back).astype(BF16)
            out_ref[:, s] = out[:out_ref.shape[0]]
            k += 1


def pre_grads(where, pre, rows, own, halves):
    vmem = pl.BlockSpec(memory_space=pltpu.VMEM)
    counts = [a.shape[1] // own for a, _ in halves]
    return pl.pallas_call(
        functools.partial(grads, counts, own),
        out_shape=jax.ShapeDtypeStruct((rows, pre.shape[1]), BF16),
        in_specs=[pl.BlockSpec(memory_space=pltpu.SMEM)] + [vmem] * (1 + 2 * len(halves)),
        out_specs=vmem,
        compiler_params=pltpu.CompilerParams(vmem_limit_bytes=40 * 2**20),
    )(where, pre, *[x for pair in halves for x in pair])


def finish(side, own_ref, came_ref, error_ref, left_ref, right_ref, out_ref):
    rows, feat = error_ref.shape
    width = own_ref.shape[1]
    start = feat - width
    first = side[0] == 0
    left = left_ref[...]
    for base, top, turn in ((0, start, True), (start, feat, False)):
        for lo in range(base, top, 512):
            part = slice(lo, min(top, lo + 512))
            at = slice(part.start - base, part.stop - base)
            mine, came = own_ref[:, at], came_ref[:, at].astype(F32)
            grad = jnp.where(first, mine, came) if turn else jnp.where(first, came, mine)
            out_ref[:, part] = grad[:rows] + error_ref[:, part] - dot(left, right_ref[:, part], 1, 0)


def new_errors(side, own, came, error, left, right):
    vmem = pl.BlockSpec(memory_space=pltpu.VMEM)
    return pl.pallas_call(
        finish,
        out_shape=jax.ShapeDtypeStruct(error.shape, F32),
        in_specs=[pl.BlockSpec(memory_space=pltpu.SMEM)] + [vmem] * 5,
        out_specs=vmem,
        compiler_params=pltpu.CompilerParams(vmem_limit_bytes=40 * 2**20),
    )(side, own, came, error, left, right)


def tie(*values):
    return lax.optimization_barrier(values)


def shards(sizes, pre_act, out_grad, weight, error, q_init):
    hi = lax.Precision.HIGHEST
    nz, nc, ny, nx = sizes
    groups = nz * nc
    mp = ny * nx
    rank = q_init.shape[1]
    half = rank // 2
    hid, toks = pre_act.shape
    own, feat = out_grad.shape
    error = error[0]
    core = lax.axis_index("core")

    iy, ix = lax.axis_index("y"), lax.axis_index("x")

    side = (ix ^ (ix >> 1)) & 1
    start = feat // 256 * 128
    width = feat - start
    rows = -(-hid // 16) * 16
    og = out_grad.T
    og_give = jnp.where(side == 0, og[start:], og[:width])
    og_mine = jnp.where(side == 0, og[:width], og[start:])
    pre_pad = jnp.pad(pre_act, ((0, rows - hid), (0, 0)))
    w_pad = jnp.pad(weight, ((0, rows - hid), (0, 0)))
    w_first, w_last = w_pad[:, :width], w_pad[:, start:]
    w_last = jnp.where(jnp.arange(width) < width - start, jnp.zeros_like(w_last), w_last)
    w_mine = jnp.where(side == 0, w_first, w_last)
    w_give = jnp.where(side == 0, w_last, w_first)

    def spot(keys):
        out = []
        for j, dy in keys:
            at = (nx - 1 - ix) if j else ix
            row = ((iy + dy) & (ny - 1)) * nx
            out += [row + at, row + (at ^ 1)]
        return jnp.stack(out)

    def around(x):
        return shift(x, "y", 1), shift(x, "y", -1), peer(x)

    def beyond(up, down, over):
        return shift(up, "y", 1), peer(up), shift(over, "y", -1)

    a0, b0 = og_mine, partner(og_give)
    a1 = around(a0)

    act = gelu16(pre_act)
    q3 = jnp.concatenate(split(q_init, 3), axis=1)
    y = fold(dot(q3, out_grad, 0, 1), 3)
    y_all, a0, b0, a1, pre_pad, w_give = tie(spread(y, MP), a0, b0, a1, pre_pad, w_give)
    b1 = around(b0)
    pre_two = (pre_pad, partner(pre_pad))
    w_two = (w_mine, partner(w_give))
    y_all = y_all.transpose(1, 0, 2).reshape(rank, toks)
    y3 = jnp.concatenate(split(y_all, 3), axis=0)
    e2 = split(error, 2)
    p_err = sum(fold(dot(q3, e, 0, 1), 3) for e in e2)
    p_local = fold(dot(y3, act, 1, 1), 3) + p_err
    p_local, b1, pre_two = tie(spread(p_local, "z"), b1, pre_two)
    a2, b2 = beyond(*a1), beyond(*b1)
    pbar = jnp.sum(p_local, axis=0)
    pbar = (pbar + other_core(pbar)) / groups

    l3 = jnp.concatenate(split(pbar, 3), axis=0)
    z_part = fold(dot(l3, act, 1, 0), 3)
    gram_part = jnp.dot(pbar, pbar.T, precision=hi)
    quarter = 128 // rank
    flat = jnp.concatenate(jnp.split(gram_part, quarter, axis=0), axis=1)
    sent = jnp.concatenate(
        [
            z_part.reshape(rank, mp, own).transpose(1, 0, 2),
            jnp.broadcast_to(flat, (mp,) + flat.shape),
        ],
        axis=1,
    )
    sent, a2, w_two = tie(sent, a2, w_two)
    a3 = peer(a2[0])
    keys = [[(0, 0), (0, 1), (0, -1), (1, 0)], [(0, 2), (1, 1), (1, -1)], [(1, 2)]]
    places = [spot(k) for k in keys]
    turns = [[x] for both in zip((a0,) + a1, (b0,) + b1) for x in both]
    keep_1, send_1, total = add_products(places[0], pre_two, w_two, turns, None)
    took = lax.all_to_all(sent, MP, 0, 0, tiled=True)
    took = jnp.sum(took, axis=0)
    z = took[:rank]
    gram = jnp.concatenate(jnp.split(took[rank:], quarter, axis=1), axis=0)

    z3 = jnp.concatenate(split(z, 3), axis=0)
    r_local = fold(dot(z3, out_grad, 1, 0), 3) + sum(fold(dot(l3, e, 1, 0), 3) for e in e2)
    low, high = r_local[:half], r_local[half:]
    keep = jnp.where(core == 0, low, high) + other_core(jnp.where(core == 0, high, low))
    r_part = lax.all_to_all(keep.reshape(nz, half // nz, feat), "z", 0, 0, tiled=True)
    r_part, b2, a3, total = tie(r_part, b2, a3, total)
    b3 = shift(b2[1], "y", 1)
    came_1 = partner(send_1)
    turns = [[x] for both in zip(a2, b2) for x in both]
    keep_2, send_2, total = add_products(places[1], pre_two, w_two, turns, total)
    r_part = jnp.sum(r_part, axis=0)
    r_part, b3, total = tie(spread(r_part, MP), b3, total)
    came_2 = partner(send_2)
    keep_3, send_3, grad_mine, grad_give = add_products(places[2], pre_two, w_two, [[a3], [b3]], total, True)
    r_part, grad_give, send_3 = tie(jnp.sum(r_part, axis=0) / groups, grad_give, send_3)
    grad_came = partner(grad_give)
    came_3 = partner(send_3)
    mine, grad_came = tie(spread(r_part, "z"), grad_came)
    mine = mine.reshape(half, feat)
    halves = [(keep_1, came_1), (keep_2, came_2), (keep_3, came_3)]
    pre_grad = pre_grads(jnp.concatenate(places), pre_pad, hid, own, halves)
    theirs = other_core(mine)
    r_all = jnp.concatenate([jnp.where(core == 0, mine, theirs), jnp.where(core == 0, theirs, mine)], axis=0)

    lower = jnp.linalg.cholesky(gram)
    inv = jax.scipy.linalg.solve_triangular(lower, jnp.eye(rank, dtype=F32), lower=True)
    q_t = jnp.dot(inv, r_all, precision=hi)
    phat = jnp.dot(inv, pbar, precision=hi)

    ph, pw = split(phat, 2)
    qh, ql = split(q_t, 2)
    left = jnp.concatenate([ph, ph, pw], axis=0).T
    right = jnp.concatenate([qh, ql, qh], axis=0)
    new_error = new_errors(side.reshape(1), grad_mine, grad_came, error, left, right)[None]
    return (pre_grad, new_error, q_t.T)


def solution(mesh):
    sizes = (mesh.shape["replica"] // 2, 2, 4, mesh.shape["mp"] // 4)
    grid = Mesh(mesh.devices.reshape(sizes), ALL)

    def run(*args):
        return shards(sizes, *args)

    return jax.shard_map(
        run,
        mesh=grid,
        in_specs=(
            P(MP, ("z", "core")),
            P(ALL, None),
            P(MP, None),
            P(("z", "core"), MP, None),
            P(),
        ),
        out_specs=(P(MP, ("z", "core")), P(("z", "core"), MP, None), P()),
        check_vma=False,
    )
```

```python
import functools

import jax
import jax.numpy as jnp
from jax import lax
from jax.experimental import pallas as pl
from jax.experimental.pallas import tpu as pltpu
from jax.sharding import Mesh, PartitionSpec as P

F32 = jnp.float32
BF16 = jnp.bfloat16
MP = ("y", "x")
ALL = ("z", "core", "y", "x")


def gelu_back(pre, grad):
    _, pull = jax.vjp(jax.nn.gelu, pre)
    return pull(grad)[0]


def gelu16(pre):
    return jax.nn.gelu(pre.astype(F32)).astype(BF16)


def split(x, parts):
    out = []
    for _ in range(parts):
        top = lax.reduce_precision(x, 8, 7)
        out.append(top.astype(BF16))
        x = x - top
    return out


def dot(a, b, ca, cb):
    return lax.dot_general(a, b, (((ca,), (cb,)), ((), ())), preferred_element_type=F32)


def fold(x, parts, axis=0):
    n = x.shape[axis] // parts
    return sum(lax.slice_in_dim(x, i * n, (i + 1) * n, axis=axis) for i in range(parts))


def spread(x, axis):
    n = lax.axis_size(axis)
    return lax.all_to_all(jnp.broadcast_to(x, (n,) + x.shape), axis, 0, 0, tiled=True)


def other_core(x):
    return lax.ppermute(x, "core", [(0, 1), (1, 0)])


def shift(x, axis, step):
    n = lax.axis_size(axis)
    return lax.ppermute(x, axis, [((i + step) % n, i) for i in range(n)])


def partner(x):
    return lax.ppermute(x, "x", [(i, i ^ 1) for i in range(lax.axis_size("x"))])


def peer(x):
    n = lax.axis_size("x")
    return lax.ppermute(x, "x", [(i, n - 1 - i) for i in range(n)])


def products(n, first, last, where, pre_a, pre_b, w_a, w_b, *refs):
    refs = list(refs)
    blocks = [[refs.pop(0) for _ in range(k)] for k in n]
    total = None if first else refs.pop(0)
    keep_ref, send_ref, *outs = refs
    own = blocks[0][0].shape[1]
    rows, feat = w_a.shape
    spots = [pl.ds(pl.multiple_of(where[i] * own, own), own) for i in range(len(blocks))]
    pre = [jnp.concatenate([p[:, s] for s in spots], axis=1) for p in (pre_a, pre_b)]
    act = gelu16(jnp.concatenate(pre, axis=0))
    back = jnp.zeros(act.shape, F32)
    edges, at = [], 0
    for ref in blocks[0]:
        edges.append(at)
        at += ref.shape[0]
    for k, edge in enumerate(edges):
        size = blocks[0][k].shape[0]
        for lo in range(0, size, 512):
            here = slice(lo, min(size, lo + 512))
            part = slice(edge + here.start, edge + here.stop)
            piece = jnp.concatenate([b[k][here, :] for b in blocks], axis=1)
            left = jnp.concatenate([w_a[:, part], w_b[:, part]], axis=0)
            back = back + dot(left, piece, 1, 0)
            more = dot(act, piece, 1, 1)
            if total is not None:
                more = more + total[:, part]
            if last:
                outs[0][:, part] = more[:rows]
                outs[1][:, part] = more[rows:].astype(BF16)
            else:
                outs[0][:, part] = more
    keep_ref[...] = back[:rows]
    send_ref[...] = back[rows:].astype(BF16)


def add_products(where, pre, weight, blocks, total, last=False):
    vmem = pl.BlockSpec(memory_space=pltpu.VMEM)
    rows, feat = weight[0].shape
    toks = sum(b[0].shape[1] for b in blocks)
    flat = [x for b in blocks for x in b] + ([] if total is None else [total])
    shape = jax.ShapeDtypeStruct
    out = [shape((rows, toks), F32), shape((rows, toks), BF16)]
    if last:
        out += [shape((rows, feat), F32), shape((rows, feat), BF16)]
    else:
        out += [shape((2 * rows, feat), F32)]
    return pl.pallas_call(
        functools.partial(products, [len(b) for b in blocks], total is None, last),
        out_shape=out,
        in_specs=[pl.BlockSpec(memory_space=pltpu.SMEM)] + [vmem] * (4 + len(flat)),
        out_specs=[vmem] * len(out),
        compiler_params=pltpu.CompilerParams(vmem_limit_bytes=20 * 2**20),
    )(where, *pre, *weight, *flat)


def grads(counts, own, where, pre_ref, *refs):
    *halves, out_ref = refs
    k = 0
    for n, keep, came in zip(counts, halves[::2], halves[1::2]):
        for i in range(n):
            s = pl.ds(pl.multiple_of(where[k] * own, own), own)
            j = i ^ 1
            back = keep[:, i * own:(i + 1) * own] + came[:, j * own:(j + 1) * own].astype(F32)
            out = gelu_back(pre_ref[:, s].astype(F32), back).astype(BF16)
            out_ref[:, s] = out[:out_ref.shape[0]]
            k += 1


def pre_grads(where, pre, rows, own, halves):
    vmem = pl.BlockSpec(memory_space=pltpu.VMEM)
    counts = [a.shape[1] // own for a, _ in halves]
    return pl.pallas_call(
        functools.partial(grads, counts, own),
        out_shape=jax.ShapeDtypeStruct((rows, pre.shape[1]), BF16),
        in_specs=[pl.BlockSpec(memory_space=pltpu.SMEM)] + [vmem] * (1 + 2 * len(halves)),
        out_specs=vmem,
        compiler_params=pltpu.CompilerParams(vmem_limit_bytes=20 * 2**20),
    )(where, pre, *[x for pair in halves for x in pair])


def finish(side, own_ref, came_ref, error_ref, left_ref, right_ref, out_ref):
    rows, _, feat = error_ref.shape
    width = own_ref.shape[1]
    start = feat - width
    first = side[0] == 0
    left = left_ref[...]
    for base, top, turn in ((0, start, True), (start, feat, False)):
        for lo in range(base, top, 512):
            part = slice(lo, min(top, lo + 512))
            at = slice(part.start - base, part.stop - base)
            mine, came = own_ref[:, at], came_ref[:, at].astype(F32)
            grad = jnp.where(first, mine, came) if turn else jnp.where(first, came, mine)
            out_ref[:, 0, part] = grad[:rows] + error_ref[:, 0, part] - dot(left, right_ref[:, part], 1, 0)


def new_errors(side, own, came, error, left, right):
    vmem = pl.BlockSpec(memory_space=pltpu.VMEM)
    return pl.pallas_call(
        finish,
        out_shape=jax.ShapeDtypeStruct(error.shape, F32),
        in_specs=[pl.BlockSpec(memory_space=pltpu.SMEM)] + [vmem] * 5,
        out_specs=vmem,
        compiler_params=pltpu.CompilerParams(vmem_limit_bytes=20 * 2**20),
    )(side, own, came, error, left, right)


def right_rows(z_ref, og_ref, more_ref, out_ref):
    rank, feat = out_ref.shape
    z = z_ref[...]
    for lo in range(0, feat, 512):
        part = slice(lo, min(feat, lo + 512))
        out_ref[:, part] = fold(dot(z, og_ref[part, :], 1, 1), 3) + more_ref[:, part]


def right_factor(z3, og, more):
    vmem = pl.BlockSpec(memory_space=pltpu.VMEM)
    return pl.pallas_call(
        right_rows,
        out_shape=jax.ShapeDtypeStruct(more.shape, F32),
        in_specs=[vmem] * 3,
        out_specs=vmem,
        compiler_params=pltpu.CompilerParams(vmem_limit_bytes=12 * 2**20),
    )(z3, og, more)


def tie(*values):
    return lax.optimization_barrier(values)


def shards(sizes, pre_act, out_grad, weight, error, q_init):
    hi = lax.Precision.HIGHEST
    nz, nc, ny, nx = sizes
    groups = nz * nc
    mp = ny * nx
    rank = q_init.shape[1]
    half = rank // 2
    hid, toks = pre_act.shape
    own, feat = out_grad.shape
    error = error[0]
    core = lax.axis_index("core")

    iy, ix = lax.axis_index("y"), lax.axis_index("x")

    side = (ix ^ (ix >> 1)) & 1
    start = feat // 256 * 128
    width = feat - start
    rows = -(-hid // 16) * 16
    og = out_grad.T
    og_give = jnp.where(side == 0, og[start:], og[:width])
    og_mine = jnp.where(side == 0, og[:width], og[start:])
    pre_pad = jnp.pad(pre_act, ((0, rows - hid), (0, 0)))
    w_pad = jnp.pad(weight, ((0, rows - hid), (0, 0)))
    w_first, w_last = w_pad[:, :width], w_pad[:, start:]
    w_last = jnp.where(jnp.arange(width) < width - start, jnp.zeros_like(w_last), w_last)
    w_mine = jnp.where(side == 0, w_first, w_last)
    w_give = jnp.where(side == 0, w_last, w_first)

    def spot(keys):
        out = []
        for j, dy in keys:
            at = (nx - 1 - ix) if j else ix
            row = ((iy + dy) & (ny - 1)) * nx
            out += [row + at, row + (at ^ 1)]
        return jnp.stack(out)

    def around(x):
        return shift(x, "y", 1), shift(x, "y", -1), peer(x)

    def beyond(up, down, over):
        return shift(up, "y", 1), peer(up), shift(over, "y", -1)

    a0, b0 = og_mine, partner(og_give)
    a1 = around(a0)

    act = gelu16(pre_act)
    q3 = jnp.concatenate(split(q_init, 3), axis=1)
    y = fold(dot(q3, out_grad, 0, 1), 3)
    y_all, a0, b0, a1, pre_pad, w_give = tie(spread(y, MP), a0, b0, a1, pre_pad, w_give)
    b1 = around(b0)
    pre_two = (pre_pad, partner(pre_pad))
    w_two = (w_mine, partner(w_give))
    a2 = beyond(*a1)
    y_all = y_all.transpose(1, 0, 2).reshape(rank, toks)
    y3 = jnp.concatenate(split(y_all, 3), axis=0)
    e2 = split(error, 2)
    p_err = sum(fold(dot(q3, e, 0, 1), 3) for e in e2)
    p_local = fold(dot(y3, act, 1, 1), 3) + p_err
    p_local, b1, a2, pre_two = tie(spread(p_local, "z"), b1, a2, pre_two)
    b2 = beyond(*b1)
    a3 = peer(a2[0])
    pbar = jnp.sum(p_local, axis=0)
    pbar = (pbar + other_core(pbar)) / groups

    l3 = jnp.concatenate(split(pbar, 3), axis=0)
    r_error = sum(fold(dot(l3, e, 1, 0), 3) for e in e2)
    z_part = fold(dot(l3, act, 1, 0), 3)
    gram_part = jnp.dot(pbar, pbar.T, precision=hi)
    quarter = 128 // rank
    flat = jnp.concatenate(jnp.split(gram_part, quarter, axis=0), axis=1)
    sent = jnp.concatenate(
        [
            z_part.reshape(rank, mp, own).transpose(1, 0, 2),
            jnp.broadcast_to(flat, (mp,) + flat.shape),
        ],
        axis=1,
    )
    keys = [[(0, 0), (0, 1), (0, -1), (1, 0)], [(0, 2), (1, 1), (1, -1)], [(1, 2)]]
    places = [spot(k) for k in keys]
    turns = [[x] for both in zip((a0,) + a1, (b0,) + b1) for x in both]
    took, b2, w_two = tie(lax.all_to_all(sent, MP, 0, 0, tiled=True), b2, w_two)
    b3 = shift(b2[1], "y", 1)
    keep_1, send_1, total = add_products(places[0], pre_two, w_two, turns, None)
    took = jnp.sum(took, axis=0)
    z = took[:rank]
    gram = jnp.concatenate(jnp.split(took[rank:], quarter, axis=1), axis=0)

    z3 = jnp.concatenate(split(z, 3), axis=0)
    r_local = right_factor(z3, og, r_error)
    low, high = r_local[:half], r_local[half:]
    keep = jnp.where(core == 0, low, high) + other_core(jnp.where(core == 0, high, low))
    r_part = lax.all_to_all(keep.reshape(nz, half // nz, feat), "z", 0, 0, tiled=True)
    r_part, a3, b3, total, send_1 = tie(r_part, a3, b3, total, send_1)
    came_1 = partner(send_1)
    turns = [[x] for both in zip(a2, b2) for x in both]
    keep_2, send_2, total = add_products(places[1], pre_two, w_two, turns, total)
    keep_3, send_3, grad_mine, grad_give = add_products(places[2], pre_two, w_two, [[a3], [b3]], total, True)
    r_part = jnp.sum(r_part, axis=0)
    r_part, grad_give, send_2, send_3 = tie(spread(r_part, MP), grad_give, send_2, send_3)
    came_2, came_3, grad_came = partner(send_2), partner(send_3), partner(grad_give)
    r_part = jnp.sum(r_part, axis=0) / groups
    halves = [(keep_1, came_1), (keep_2, came_2), (keep_3, came_3)]
    pre_grad = pre_grads(jnp.concatenate(places), pre_pad, hid, own, halves)
    mine, grad_came, pre_grad = tie(spread(r_part, "z"), grad_came, pre_grad)
    mine = mine.reshape(half, feat)
    theirs = other_core(mine)
    r_all = jnp.concatenate([jnp.where(core == 0, mine, theirs), jnp.where(core == 0, theirs, mine)], axis=0)

    lower = jnp.linalg.cholesky(gram)
    inv = jax.scipy.linalg.solve_triangular(lower, jnp.eye(rank, dtype=F32), lower=True)
    q_t = jnp.dot(inv, r_all, precision=hi)
    phat = jnp.dot(inv, pbar, precision=hi)

    ph, pw = split(phat, 2)
    qh, ql = split(q_t, 2)
    left = jnp.concatenate([ph, ph, pw], axis=0).T
    right = jnp.concatenate([qh, ql, qh], axis=0)
    new_error = new_errors(side.reshape(1), grad_mine, grad_came, error[:, None], left, right)
    new_error = new_error.transpose(1, 0, 2)
    return (pre_grad, new_error, q_t.T)


def solution(mesh):
    sizes = (mesh.shape["replica"] // 2, 2, 4, mesh.shape["mp"] // 4)
    grid = Mesh(mesh.devices.reshape(sizes), ALL)

    def run(*args):
        return shards(sizes, *args)

    return jax.shard_map(
        run,
        mesh=grid,
        in_specs=(
            P(MP, ("z", "core")),
            P(ALL, None),
            P(MP, None),
            P(("z", "core"), MP, None),
            P(),
        ),
        out_specs=(P(MP, ("z", "core")), P(("z", "core"), MP, None), P()),
        check_vma=False,
    )
```

```python
import functools

import jax
import jax.numpy as jnp
from jax import lax
from jax.experimental import pallas as pl
from jax.experimental.pallas import tpu as pltpu
from jax.sharding import Mesh, PartitionSpec as P

F32 = jnp.float32
BF16 = jnp.bfloat16
MP = ("y", "x")
ALL = ("z", "core", "y", "x")


def gelu_back(pre, grad):
    _, pull = jax.vjp(jax.nn.gelu, pre)
    return pull(grad)[0]


def gelu16(pre):
    return jax.nn.gelu(pre.astype(F32)).astype(BF16)


def split(x, parts):
    out = []
    for _ in range(parts):
        top = lax.reduce_precision(x, 8, 7)
        out.append(top.astype(BF16))
        x = x - top
    return out


def dot(a, b, ca, cb):
    return lax.dot_general(a, b, (((ca,), (cb,)), ((), ())), preferred_element_type=F32)


def fold(x, parts, axis=0):
    n = x.shape[axis] // parts
    return sum(lax.slice_in_dim(x, i * n, (i + 1) * n, axis=axis) for i in range(parts))


def spread(x, axis):
    n = lax.axis_size(axis)
    return lax.all_to_all(jnp.broadcast_to(x, (n,) + x.shape), axis, 0, 0, tiled=True)


def other_core(x):
    return lax.ppermute(x, "core", [(0, 1), (1, 0)])


def shift(x, axis, step):
    n = lax.axis_size(axis)
    return lax.ppermute(x, axis, [((i + step) % n, i) for i in range(n)])


def partner(x):
    return lax.ppermute(x, "x", [(i, i ^ 1) for i in range(lax.axis_size("x"))])


def peer(x):
    n = lax.axis_size("x")
    return lax.ppermute(x, "x", [(i, n - 1 - i) for i in range(n)])


def products(n, first, last, where, pre_a, pre_b, w_a, w_b, *refs):
    refs = list(refs)
    blocks = [[refs.pop(0) for _ in range(k)] for k in n]
    total = None if first else refs.pop(0)
    keep_ref, send_ref, *outs = refs
    own = blocks[0][0].shape[1]
    rows, feat = w_a.shape
    spots = [pl.ds(pl.multiple_of(where[i] * own, own), own) for i in range(len(blocks))]
    pre = [jnp.concatenate([p[:, s] for s in spots], axis=1) for p in (pre_a, pre_b)]
    act = gelu16(jnp.concatenate(pre, axis=0))
    back = jnp.zeros(act.shape, F32)
    edges, at = [], 0
    for ref in blocks[0]:
        edges.append(at)
        at += ref.shape[0]
    for k, edge in enumerate(edges):
        size = blocks[0][k].shape[0]
        for lo in range(0, size, 512):
            here = slice(lo, min(size, lo + 512))
            part = slice(edge + here.start, edge + here.stop)
            piece = jnp.concatenate([b[k][here, :] for b in blocks], axis=1)
            left = jnp.concatenate([w_a[:, part], w_b[:, part]], axis=0)
            back = back + dot(left, piece, 1, 0)
            more = dot(act, piece, 1, 1)
            if total is not None:
                more = more + total[:, part]
            if last:
                outs[0][:, part] = more[:rows]
                outs[1][:, part] = more[rows:].astype(BF16)
            else:
                outs[0][:, part] = more
    keep_ref[...] = back[:rows]
    send_ref[...] = back[rows:].astype(BF16)


def add_products(where, pre, weight, blocks, total, last=False):
    vmem = pl.BlockSpec(memory_space=pltpu.VMEM)
    rows, feat = weight[0].shape
    toks = sum(b[0].shape[1] for b in blocks)
    flat = [x for b in blocks for x in b] + ([] if total is None else [total])
    shape = jax.ShapeDtypeStruct
    out = [shape((rows, toks), F32), shape((rows, toks), BF16)]
    if last:
        out += [shape((rows, feat), F32), shape((rows, feat), BF16)]
    else:
        out += [shape((2 * rows, feat), F32)]
    return pl.pallas_call(
        functools.partial(products, [len(b) for b in blocks], total is None, last),
        out_shape=out,
        in_specs=[pl.BlockSpec(memory_space=pltpu.SMEM)] + [vmem] * (4 + len(flat)),
        out_specs=[vmem] * len(out),
        compiler_params=pltpu.CompilerParams(vmem_limit_bytes=12 * 2**20),
    )(where, *pre, *weight, *flat)


def grads(counts, own, where, pre_ref, *refs):
    *halves, out_ref = refs
    k = 0
    for n, keep, came in zip(counts, halves[::2], halves[1::2]):
        for i in range(n):
            s = pl.ds(pl.multiple_of(where[k] * own, own), own)
            back = keep[:, i * own:(i + 1) * own] + came[:, i * own:(i + 1) * own].astype(F32)
            out = gelu_back(pre_ref[:, s].astype(F32), back).astype(BF16)
            out_ref[:, s] = out[:out_ref.shape[0]]
            k += 1


def pre_grads(where, pre, rows, own, halves):
    vmem = pl.BlockSpec(memory_space=pltpu.VMEM)
    counts = [a.shape[1] // own for a, _ in halves]
    return pl.pallas_call(
        functools.partial(grads, counts, own),
        out_shape=jax.ShapeDtypeStruct((rows, pre.shape[1]), BF16),
        in_specs=[pl.BlockSpec(memory_space=pltpu.SMEM)] + [vmem] * (1 + 2 * len(halves)),
        out_specs=vmem,
        compiler_params=pltpu.CompilerParams(vmem_limit_bytes=12 * 2**20),
    )(where, pre, *[x for pair in halves for x in pair])


def finish(side, own_ref, came_ref, error_ref, left_ref, right_ref, out_ref):
    rows, _, feat = error_ref.shape
    width = own_ref.shape[1]
    start = feat - width
    first = side[0] == 0
    left = left_ref[...]
    for base, top, turn in ((0, start, True), (start, feat, False)):
        for lo in range(base, top, 512):
            part = slice(lo, min(top, lo + 512))
            at = slice(part.start - base, part.stop - base)
            mine, came = own_ref[:, at], came_ref[:, at].astype(F32)
            grad = jnp.where(first, mine, came) if turn else jnp.where(first, came, mine)
            out_ref[:, 0, part] = grad[:rows] + error_ref[:, 0, part] - dot(left, right_ref[:, part], 1, 0)


def new_errors(side, own, came, error, left, right):
    vmem = pl.BlockSpec(memory_space=pltpu.VMEM)
    return pl.pallas_call(
        finish,
        out_shape=jax.ShapeDtypeStruct(error.shape, F32),
        in_specs=[pl.BlockSpec(memory_space=pltpu.SMEM)] + [vmem] * 5,
        out_specs=vmem,
        compiler_params=pltpu.CompilerParams(vmem_limit_bytes=12 * 2**20),
    )(side, own, came, error, left, right)


def right_rows(z_ref, og_ref, more_ref, out_ref):
    rank, feat = out_ref.shape
    z = z_ref[...]
    for lo in range(0, feat, 512):
        part = slice(lo, min(feat, lo + 512))
        out_ref[:, part] = fold(dot(z, og_ref[part, :], 1, 1), 3) + more_ref[:, part]


def right_factor(z3, og, more):
    vmem = pl.BlockSpec(memory_space=pltpu.VMEM)
    return pl.pallas_call(
        right_rows,
        out_shape=jax.ShapeDtypeStruct(more.shape, F32),
        in_specs=[vmem] * 3,
        out_specs=vmem,
        compiler_params=pltpu.CompilerParams(vmem_limit_bytes=12 * 2**20),
    )(z3, og, more)


def tie(*values):
    return lax.optimization_barrier(values)


def shards(sizes, pre_act, out_grad, weight, error, q_init):
    hi = lax.Precision.HIGHEST
    nz, nc, ny, nx = sizes
    groups = nz * nc
    mp = ny * nx
    rank = q_init.shape[1]
    half = rank // 2
    hid, toks = pre_act.shape
    own, feat = out_grad.shape
    error = error[0]
    core = lax.axis_index("core")

    iy, ix = lax.axis_index("y"), lax.axis_index("x")

    side = (ix ^ (ix >> 1)) & 1
    start = feat // 256 * 128
    width = feat - start
    rows = -(-hid // 16) * 16
    og = out_grad.T
    og_give = jnp.where(side == 0, og[start:], og[:width])
    og_mine = jnp.where(side == 0, og[:width], og[start:])
    pre_pad = jnp.pad(pre_act, ((0, rows - hid), (0, 0)))
    w_pad = jnp.pad(weight, ((0, rows - hid), (0, 0)))
    w_first, w_last = w_pad[:, :width], w_pad[:, start:]
    w_last = jnp.where(jnp.arange(width) < width - start, jnp.zeros_like(w_last), w_last)
    w_mine = jnp.where(side == 0, w_first, w_last)
    w_give = jnp.where(side == 0, w_last, w_first)

    def spot(keys):
        return jnp.stack([((iy + dy) & (ny - 1)) * (nx // 2) + ((ix >> 1) ^ j) for j, dy in keys])

    def around(x):
        return shift(x, "y", 1), shift(x, "y", -1), peer(x)

    def beyond(up, down, over):
        return shift(up, "y", 1), peer(up), shift(over, "y", -1)

    def corner(far, over_up, over_down):
        cut = (width // 3 + 64) // 128 * 128
        return (
            peer(far[:cut]),
            shift(over_up[cut:2 * cut], "y", 1),
            shift(over_down[2 * cut:], "y", -1),
        )

    og_came = partner(og_give)
    pair = 2 * own

    act = gelu16(pre_act)
    q3 = jnp.concatenate(split(q_init, 3), axis=1)
    y = fold(dot(q3, out_grad, 0, 1), 3)
    y_all, og_mine, og_came, pre_pad, w_give = tie(spread(y, MP), og_mine, og_came, pre_pad, w_give)
    below = jnp.where((ix & 1) == 0, og_mine, og_came)
    above = jnp.where((ix & 1) == 0, og_came, og_mine)
    block = jnp.concatenate([below, above], axis=1)
    one = around(block)
    pre_two = (pre_pad, partner(pre_pad))
    w_two = (w_mine, partner(w_give))
    y_all = y_all.transpose(1, 0, 2).reshape(rank, toks)
    y3 = jnp.concatenate(split(y_all, 3), axis=0)
    e2 = split(error, 2)
    p_err = sum(fold(dot(q3, e, 0, 1), 3) for e in e2)
    p_local = fold(dot(y3, act, 1, 1), 3) + p_err
    pbar = jnp.sum(spread(p_local, "z"), axis=0)
    pbar, one, pre_two = tie((pbar + other_core(pbar)) / groups, one, pre_two)

    l3 = jnp.concatenate(split(pbar, 3), axis=0)
    r_error = sum(fold(dot(l3, e, 1, 0), 3) for e in e2)
    z_part = fold(dot(l3, act, 1, 0), 3)
    gram_part = jnp.dot(pbar, pbar.T, precision=hi)
    quarter = 128 // rank
    flat = jnp.concatenate(jnp.split(gram_part, quarter, axis=0), axis=1)
    sent = jnp.concatenate(
        [
            z_part.reshape(rank, mp, own).transpose(1, 0, 2),
            jnp.broadcast_to(flat, (mp,) + flat.shape),
        ],
        axis=1,
    )
    keys = [[(0, 0), (0, 1), (0, -1), (1, 0)], [(0, 2), (1, 1), (1, -1)], [(1, 2)]]
    places = [spot(k) for k in keys]
    took, one, w_two = tie(lax.all_to_all(sent, MP, 0, 0, tiled=True), one, w_two)
    two = beyond(*one)
    keep_1, send_1, total = add_products(places[0], pre_two, w_two, [[x] for x in (block,) + one], None)
    took = jnp.sum(took, axis=0)
    z = took[:rank]
    gram = jnp.concatenate(jnp.split(took[rank:], quarter, axis=1), axis=0)

    z3 = jnp.concatenate(split(z, 3), axis=0)
    r_local = right_factor(z3, og, r_error)
    low, high = r_local[:half], r_local[half:]
    keep = jnp.where(core == 0, low, high) + other_core(jnp.where(core == 0, high, low))
    r_part = lax.all_to_all(keep.reshape(nz, half // nz, feat), "z", 0, 0, tiled=True)
    r_part, two, total, send_1 = tie(r_part, two, total, send_1)
    last = corner(*two)
    came_1 = partner(send_1)
    keep_2, send_2, total = add_products(places[1], pre_two, w_two, [[x] for x in two], total)
    came_2 = partner(send_2)
    r_part = jnp.sum(r_part, axis=0)
    r_part, last, total, came_1, came_2 = tie(spread(r_part, MP), last, total, came_1, came_2)
    keep_3, send_3, grad_mine, grad_give = add_products(places[2], pre_two, w_two, [list(last)], total, True)
    came_3 = partner(send_3)
    r_part = jnp.sum(r_part, axis=0) / groups
    r_part, grad_give = tie(r_part, grad_give)
    grad_came = partner(grad_give)
    halves = [(keep_1, came_1), (keep_2, came_2), (keep_3, came_3)]
    pre_grad = pre_grads(jnp.concatenate(places), pre_pad, hid, pair, halves)
    mine, grad_came, pre_grad = tie(spread(r_part, "z"), grad_came, pre_grad)
    mine = mine.reshape(half, feat)
    theirs = other_core(mine)
    r_all = jnp.concatenate([jnp.where(core == 0, mine, theirs), jnp.where(core == 0, theirs, mine)], axis=0)

    lower = jnp.linalg.cholesky(gram)
    inv = jax.scipy.linalg.solve_triangular(lower, jnp.eye(rank, dtype=F32), lower=True)
    q_t = jnp.dot(inv, r_all, precision=hi)
    phat = jnp.dot(inv, pbar, precision=hi)

    ph, pw = split(phat, 2)
    qh, ql = split(q_t, 2)
    left = jnp.concatenate([ph, ph, pw], axis=0).T
    right = jnp.concatenate([qh, ql, qh], axis=0)
    new_error = new_errors(side.reshape(1), grad_mine, grad_came, error[:, None], left, right)
    new_error = new_error.transpose(1, 0, 2)
    return (pre_grad, new_error, q_t.T)


def solution(mesh):
    sizes = (mesh.shape["replica"] // 2, 2, 4, mesh.shape["mp"] // 4)
    grid = Mesh(mesh.devices.reshape(sizes), ALL)

    def run(*args):
        return shards(sizes, *args)

    return jax.shard_map(
        run,
        mesh=grid,
        in_specs=(
            P(MP, ("z", "core")),
            P(ALL, None),
            P(MP, None),
            P(("z", "core"), MP, None),
            P(),
        ),
        out_specs=(P(MP, ("z", "core")), P(("z", "core"), MP, None), P()),
        check_vma=False,
    )
```

```python
import functools

import jax
import jax.numpy as jnp
from jax import lax
from jax.experimental import pallas as pl
from jax.experimental.pallas import tpu as pltpu
from jax.sharding import Mesh, PartitionSpec as P

F32 = jnp.float32
BF16 = jnp.bfloat16
MP = ("y", "x")
ALL = ("z", "core", "y", "x")


def gelu_back(pre, grad):
    _, pull = jax.vjp(jax.nn.gelu, pre)
    return pull(grad)[0]


def gelu16(pre):
    return jax.nn.gelu(pre.astype(F32)).astype(BF16)


def split(x, parts):
    out = []
    for _ in range(parts):
        top = lax.reduce_precision(x, 8, 7)
        out.append(top.astype(BF16))
        x = x - top
    return out


def dot(a, b, ca, cb):
    return lax.dot_general(a, b, (((ca,), (cb,)), ((), ())), preferred_element_type=F32)


def fold(x, parts, axis=0):
    n = x.shape[axis] // parts
    return sum(lax.slice_in_dim(x, i * n, (i + 1) * n, axis=axis) for i in range(parts))


def spread(x, axis):
    n = lax.axis_size(axis)
    return lax.all_to_all(jnp.broadcast_to(x, (n,) + x.shape), axis, 0, 0, tiled=True)


def other_core(x):
    return lax.ppermute(x, "core", [(0, 1), (1, 0)])


def shift(x, axis, step):
    n = lax.axis_size(axis)
    return lax.ppermute(x, axis, [((i + step) % n, i) for i in range(n)])


def products(n, where, pre_ref, weight_ref, *refs):
    blocks, held, (mat_ref, grad_ref) = refs[:n], refs[n:-2], refs[-2:]
    if held:
        grad_ref[...] = held[1][...]
    own = blocks[0].shape[1]
    spots = [pl.ds(pl.multiple_of(where[i] * own, own), own) for i in range(n)]
    pre = jnp.concatenate([pre_ref[:, s] for s in spots], axis=1).astype(F32)
    act, pull = jax.vjp(jax.nn.gelu, pre)
    act = act.astype(BF16)
    feat = weight_ref.shape[1]
    back = jnp.zeros(pre.shape, F32)
    for lo in range(0, feat, 512):
        part = slice(lo, min(feat, lo + 512))
        piece = jnp.concatenate([b[part, :] for b in blocks], axis=1)
        back = back + dot(weight_ref[:, part], piece, 1, 0)
        more = dot(act, piece, 1, 1)
        mat_ref[:, part] = more + held[0][:, part] if held else more
    out = pull(back)[0].astype(BF16)
    for i, s in enumerate(spots):
        grad_ref[:, s] = out[:, i * own:(i + 1) * own]


def add_products(where, pre_act, weight, blocks, held):
    vmem = pl.BlockSpec(memory_space=pltpu.VMEM)
    n = len(blocks)
    mat = jax.ShapeDtypeStruct(weight.shape, F32)
    return pl.pallas_call(
        functools.partial(products, n),
        out_shape=(mat, jax.ShapeDtypeStruct(pre_act.shape, BF16)),
        in_specs=[pl.BlockSpec(memory_space=pltpu.SMEM)] + [vmem] * (n + 2 + len(held)),
        out_specs=(vmem, vmem),
        input_output_aliases={n + 3: 0, n + 4: 1} if held else {},
        compiler_params=pltpu.CompilerParams(vmem_limit_bytes=12 * 2**20),
    )(where, pre_act, weight, *blocks, *held)


def finish(mat_ref, error_ref, left_ref, right_ref, out_ref):
    feat = mat_ref.shape[1]
    left = left_ref[...]
    for lo in range(0, feat, 512):
        part = slice(lo, min(feat, lo + 512))
        out_ref[:, 0, part] = mat_ref[:, part] + error_ref[:, 0, part] - dot(left, right_ref[:, part], 1, 0)


def new_errors(mat, error, left, right):
    vmem = pl.BlockSpec(memory_space=pltpu.VMEM)
    return pl.pallas_call(
        finish,
        out_shape=jax.ShapeDtypeStruct(error.shape, F32),
        in_specs=[vmem] * 4,
        out_specs=vmem,
        compiler_params=pltpu.CompilerParams(vmem_limit_bytes=12 * 2**20),
    )(mat, error, left, right)


def right_rows(z_ref, og_ref, more_ref, out_ref):
    rank, feat = out_ref.shape
    z = z_ref[...]
    for lo in range(0, feat, 512):
        part = slice(lo, min(feat, lo + 512))
        out_ref[:, part] = fold(dot(z, og_ref[part, :], 1, 1), 3) + more_ref[:, part]


def right_factor(z3, og, more):
    vmem = pl.BlockSpec(memory_space=pltpu.VMEM)
    return pl.pallas_call(
        right_rows,
        out_shape=jax.ShapeDtypeStruct(more.shape, F32),
        in_specs=[vmem] * 3,
        out_specs=vmem,
        compiler_params=pltpu.CompilerParams(vmem_limit_bytes=12 * 2**20),
    )(z3, og, more)


def shards(sizes, pre_act, out_grad, weight, error, q_init):
    hi = lax.Precision.HIGHEST
    nz, nc, ny, nx = sizes
    groups = nz * nc
    mp = ny * nx
    rank = q_init.shape[1]
    half = rank // 2
    hid, toks = pre_act.shape
    own, feat = out_grad.shape
    error = error[0]
    core = lax.axis_index("core")

    og = out_grad.T
    got = {(0, 0): og}
    iy, ix = lax.axis_index("y"), lax.axis_index("x")
    state = []

    def fetch(*moves):
        new = {}
        for key, axis, step in moves:
            dy, dx = (key[0] + step, key[1]) if axis == "y" else (key[0], key[1] + step)
            new[dy % ny, dx % nx] = shift(got[key[0] % ny, key[1] % nx], axis, step)
        got.update(new)
        return list(new)

    def tie(value, keys=(), with_state=False):
        out = lax.optimization_barrier([value, [got[k] for k in keys], state if with_state else []])
        got.update(zip(keys, out[1]))
        if with_state:
            state[:] = out[2]
        return out[0]

    def use(keys):
        where = jnp.stack([((iy + dy) & (ny - 1)) * nx + ((ix + dx) & (nx - 1)) for dy, dx in keys])
        state[:] = add_products(where, pre_act, weight, [got[k] for k in keys], state)

    one = fetch(((0, 0), "x", 1), ((0, 0), "x", -1), ((0, 0), "y", 1), ((0, 0), "y", -1))

    act = gelu16(pre_act)
    q3 = jnp.concatenate(split(q_init, 3), axis=1)
    y = fold(dot(q3, out_grad, 0, 1), 3)
    y_all = tie(spread(y, MP), one)
    two = fetch(((0, 1), "y", 1), ((0, -1), "y", -1), ((1, 0), "x", -1), ((-1, 0), "x", 1))
    use([(0, 0)] + one)
    y_all = y_all.transpose(1, 0, 2).reshape(rank, toks)
    y3 = jnp.concatenate(split(y_all, 3), axis=0)
    e2 = split(error, 2)
    p_err = sum(fold(dot(q3, e, 0, 1), 3) for e in e2)
    p_local = fold(dot(y3, act, 1, 1), 3) + p_err
    pbar = jnp.sum(tie(spread(p_local, "z"), [], True), axis=0)
    pbar = tie((pbar + other_core(pbar)) / groups, two)

    l3 = jnp.concatenate(split(pbar, 3), axis=0)
    r_error = sum(fold(dot(l3, e, 1, 0), 3) for e in e2)
    z_part = fold(dot(l3, act, 1, 0), 3)
    gram_part = jnp.dot(pbar, pbar.T, precision=hi)
    side = 128 // rank
    flat = jnp.concatenate(jnp.split(gram_part, side, axis=0), axis=1)
    sent = jnp.concatenate(
        [
            z_part.reshape(rank, mp, own).transpose(1, 0, 2),
            jnp.broadcast_to(flat, (mp,) + flat.shape),
        ],
        axis=1,
    )
    took = tie(lax.all_to_all(sent, MP, 0, 0, tiled=True), two + [(0, 1), (1, 0)])
    three = fetch(((0, 1), "x", 1), ((1, 0), "y", 1), ((1, -1), "x", -1), ((-1, 1), "y", -1))
    use(two)
    took = jnp.sum(took, axis=0)
    z = took[:rank]
    gram = jnp.concatenate(jnp.split(took[rank:], side, axis=1), axis=0)

    z3 = jnp.concatenate(split(z, 3), axis=0)
    r_local = right_factor(z3, og, r_error)
    low, high = r_local[:half], r_local[half:]
    keep = jnp.where(core == 0, low, high) + other_core(jnp.where(core == 0, high, low))
    r_part = lax.all_to_all(keep.reshape(nz, half // nz, feat), "z", 0, 0, tiled=True)
    r_part = jnp.sum(tie(r_part, three + [(3, 1), (3, 3)], True), axis=0)
    four = fetch(((-1, 1), "x", 1), ((1, 2), "y", 1), ((-1, -1), "y", -1))
    use(three)
    r_part = jnp.sum(spread(r_part, MP), axis=0) / groups
    mine = tie(spread(r_part, "z"), four, True).reshape(half, feat)
    use(four)
    theirs = other_core(mine)
    r_all = jnp.concatenate([jnp.where(core == 0, mine, theirs), jnp.where(core == 0, theirs, mine)], axis=0)

    lower = jnp.linalg.cholesky(gram)
    inv = jax.scipy.linalg.solve_triangular(lower, jnp.eye(rank, dtype=F32), lower=True)
    q_t = jnp.dot(inv, r_all, precision=hi)
    phat = jnp.dot(inv, pbar, precision=hi)

    mat, pre_grad = state
    ph, pw = split(phat, 2)
    qh, ql = split(q_t, 2)
    left = jnp.concatenate([ph, ph, pw], axis=0).T
    right = jnp.concatenate([qh, ql, qh], axis=0)
    new_error = new_errors(mat, error[:, None], left, right).transpose(1, 0, 2)
    return (pre_grad, new_error, q_t.T)


def solution(mesh):
    sizes = (mesh.shape["replica"] // 2, 2, 4, mesh.shape["mp"] // 4)
    grid = Mesh(mesh.devices.reshape(sizes), ALL)

    def run(*args):
        return shards(sizes, *args)

    return jax.shard_map(
        run,
        mesh=grid,
        in_specs=(
            P(MP, ("z", "core")),
            P(ALL, None),
            P(MP, None),
            P(("z", "core"), MP, None),
            P(),
        ),
        out_specs=(P(MP, ("z", "core")), P(("z", "core"), MP, None), P()),
        check_vma=False,
    )
```

```python
import functools

import jax
import jax.numpy as jnp
from jax import lax
from jax.experimental import pallas as pl
from jax.experimental.pallas import tpu as pltpu
from jax.sharding import Mesh, PartitionSpec as P

F32 = jnp.float32
BF16 = jnp.bfloat16
MP = ("y", "x")
ALL = ("z", "core", "y", "x")


def gelu_back(pre, grad):
    _, pull = jax.vjp(jax.nn.gelu, pre)
    return pull(grad)[0]


def gelu16(pre):
    return jax.nn.gelu(pre.astype(F32)).astype(BF16)


def split(x, parts):
    out = []
    for _ in range(parts):
        top = lax.reduce_precision(x, 8, 7)
        out.append(top.astype(BF16))
        x = x - top
    return out


def dot(a, b, ca, cb):
    return lax.dot_general(a, b, (((ca,), (cb,)), ((), ())), preferred_element_type=F32)


def fold(x, parts, axis=0):
    n = x.shape[axis] // parts
    return sum(lax.slice_in_dim(x, i * n, (i + 1) * n, axis=axis) for i in range(parts))


def spread(x, axis):
    n = lax.axis_size(axis)
    return lax.all_to_all(jnp.broadcast_to(x, (n,) + x.shape), axis, 0, 0, tiled=True)


def other_core(x):
    return lax.ppermute(x, "core", [(0, 1), (1, 0)])


def shift(x, axis, step):
    n = lax.axis_size(axis)
    return lax.ppermute(x, axis, [((i + step) % n, i) for i in range(n)])


def products(n, where, pre_ref, weight_ref, *refs):
    blocks, held, (mat_ref, grad_ref, pre_buf, weight_buf, sems) = refs[:n], refs[n:-5], refs[-5:]
    fetch_pre = pltpu.make_async_copy(pre_ref, pre_buf, sems.at[0])
    fetch_weight = pltpu.make_async_copy(weight_ref, weight_buf, sems.at[1])
    fetch_pre.start()
    fetch_weight.start()
    if held:
        grad_ref[...] = held[1][...]
    own = blocks[0].shape[1]
    spots = [pl.ds(pl.multiple_of(where[i] * own, own), own) for i in range(n)]
    fetch_pre.wait()
    pre = jnp.concatenate([pre_buf[:, s] for s in spots], axis=1).astype(F32)
    act, pull = jax.vjp(jax.nn.gelu, pre)
    act = act.astype(BF16)
    fetch_weight.wait()
    feat = weight_buf.shape[1]
    back = jnp.zeros(pre.shape, F32)
    for lo in range(0, feat, 512):
        part = slice(lo, min(feat, lo + 512))
        piece = jnp.concatenate([b[part, :] for b in blocks], axis=1)
        back = back + dot(weight_buf[:, part], piece, 1, 0)
        more = dot(act, piece, 1, 1)
        mat_ref[:, part] = more + held[0][:, part] if held else more
    out = pull(back)[0].astype(BF16)
    for i, s in enumerate(spots):
        grad_ref[:, s] = out[:, i * own:(i + 1) * own]


def add_products(where, pre_act, weight, blocks, held):
    vmem = pl.BlockSpec(memory_space=pltpu.VMEM)
    n = len(blocks)
    mat = jax.ShapeDtypeStruct(weight.shape, F32)
    return pl.pallas_call(
        functools.partial(products, n),
        out_shape=(mat, jax.ShapeDtypeStruct(pre_act.shape, BF16)),
        in_specs=[pl.BlockSpec(memory_space=pltpu.SMEM)]
        + [pl.BlockSpec(memory_space=pl.ANY)] * 2
        + [vmem] * (n + len(held)),
        out_specs=(vmem, vmem),
        scratch_shapes=[
            pltpu.VMEM(pre_act.shape, BF16),
            pltpu.VMEM(weight.shape, BF16),
            pltpu.SemaphoreType.DMA((2,)),
        ],
        input_output_aliases={n + 3: 0, n + 4: 1} if held else {},
        compiler_params=pltpu.CompilerParams(vmem_limit_bytes=12 * 2**20),
    )(where, pre_act, weight, *blocks, *held)


def finish(mat_ref, error_ref, left_ref, right_ref, out_ref):
    feat = mat_ref.shape[1]
    left = left_ref[...]
    for lo in range(0, feat, 512):
        part = slice(lo, min(feat, lo + 512))
        out_ref[:, 0, part] = mat_ref[:, part] + error_ref[:, 0, part] - dot(left, right_ref[:, part], 1, 0)


def new_errors(mat, error, left, right):
    vmem = pl.BlockSpec(memory_space=pltpu.VMEM)
    return pl.pallas_call(
        finish,
        out_shape=jax.ShapeDtypeStruct(error.shape, F32),
        in_specs=[vmem] * 4,
        out_specs=vmem,
        compiler_params=pltpu.CompilerParams(vmem_limit_bytes=12 * 2**20),
    )(mat, error, left, right)


def error_rows(left_ref, error_ref, out_ref):
    left = left_ref[...]
    feat = out_ref.shape[1]
    for lo in range(0, feat, 512):
        part = slice(lo, min(feat, lo + 512))
        err = error_ref[:, 0, part]
        top = err.astype(BF16)
        low = (err - top.astype(F32)).astype(BF16)
        out_ref[:, part] = fold(dot(left, top, 1, 0) + dot(left, low, 1, 0), 3)


def error_factor(l3, error):
    vmem = pl.BlockSpec(memory_space=pltpu.VMEM)
    return pl.pallas_call(
        error_rows,
        out_shape=jax.ShapeDtypeStruct((l3.shape[0] // 3, error.shape[2]), F32),
        in_specs=[vmem] * 2,
        out_specs=vmem,
        compiler_params=pltpu.CompilerParams(vmem_limit_bytes=12 * 2**20),
    )(l3, error)


def right_rows(z_ref, og_ref, more_ref, out_ref):
    rank, feat = out_ref.shape
    z = z_ref[...]
    for lo in range(0, feat, 512):
        part = slice(lo, min(feat, lo + 512))
        out_ref[:, part] = fold(dot(z, og_ref[part, :], 1, 1), 3) + more_ref[:, part]


def right_factor(z3, og, more):
    vmem = pl.BlockSpec(memory_space=pltpu.VMEM)
    return pl.pallas_call(
        right_rows,
        out_shape=jax.ShapeDtypeStruct(more.shape, F32),
        in_specs=[vmem] * 3,
        out_specs=vmem,
        compiler_params=pltpu.CompilerParams(vmem_limit_bytes=12 * 2**20),
    )(z3, og, more)


def shards(sizes, pre_act, out_grad, weight, error, q_init):
    hi = lax.Precision.HIGHEST
    nz, nc, ny, nx = sizes
    groups = nz * nc
    mp = ny * nx
    rank = q_init.shape[1]
    half = rank // 2
    hid, toks = pre_act.shape
    own, feat = out_grad.shape
    error = error[0]
    core = lax.axis_index("core")

    og = out_grad.T
    got = {(0, 0): og}
    iy, ix = lax.axis_index("y"), lax.axis_index("x")
    state = []

    def fetch(*moves):
        new = {}
        for key, axis, step in moves:
            dy, dx = (key[0] + step, key[1]) if axis == "y" else (key[0], key[1] + step)
            new[dy % ny, dx % nx] = shift(got[key[0] % ny, key[1] % nx], axis, step)
        got.update(new)
        return list(new)

    def tie(value, keys=(), with_state=False):
        out = lax.optimization_barrier([value, [got[k] for k in keys], state if with_state else []])
        got.update(zip(keys, out[1]))
        if with_state:
            state[:] = out[2]
        return out[0]

    def use(keys):
        where = jnp.stack([((iy + dy) & (ny - 1)) * nx + ((ix + dx) & (nx - 1)) for dy, dx in keys])
        state[:] = add_products(where, pre_act, weight, [got[k] for k in keys], state)

    one = fetch(((0, 0), "x", 1), ((0, 0), "x", -1), ((0, 0), "y", 1), ((0, 0), "y", -1))

    act = gelu16(pre_act)
    q3 = jnp.concatenate(split(q_init, 3), axis=1)
    y = fold(dot(q3, out_grad, 0, 1), 3)
    y_all = tie(spread(y, MP), one)
    two = fetch(((0, 1), "y", 1), ((0, -1), "y", -1), ((1, 0), "x", -1), ((-1, 0), "x", 1))
    use([(0, 0)] + one)
    y_all = y_all.transpose(1, 0, 2).reshape(rank, toks)
    y3 = jnp.concatenate(split(y_all, 3), axis=0)
    e2 = split(error, 2)
    p_err = sum(fold(dot(q3, e, 0, 1), 3) for e in e2)
    p_local = fold(dot(y3, act, 1, 1), 3) + p_err
    pbar = jnp.sum(tie(spread(p_local, "z"), [], True), axis=0)
    pbar = tie((pbar + other_core(pbar)) / groups, two)

    l3 = jnp.concatenate(split(pbar, 3), axis=0)
    r_error = error_factor(l3, error[:, None])
    z_part = fold(dot(l3, act, 1, 0), 3)
    gram_part = jnp.dot(pbar, pbar.T, precision=hi)
    side = 128 // rank
    flat = jnp.concatenate(jnp.split(gram_part, side, axis=0), axis=1)
    sent = jnp.concatenate(
        [
            z_part.reshape(rank, mp, own).transpose(1, 0, 2),
            jnp.broadcast_to(flat, (mp,) + flat.shape),
        ],
        axis=1,
    )
    took = tie(lax.all_to_all(sent, MP, 0, 0, tiled=True), two + [(0, 1), (1, 0)])
    three = fetch(((0, 1), "x", 1), ((1, 0), "y", 1), ((1, -1), "x", -1), ((-1, 1), "y", -1))
    use(two)
    took = jnp.sum(took, axis=0)
    z = took[:rank]
    gram = jnp.concatenate(jnp.split(took[rank:], side, axis=1), axis=0)

    z3 = jnp.concatenate(split(z, 3), axis=0)
    r_local, gram = tie((right_factor(z3, og, r_error), gram))
    lower = jnp.linalg.cholesky(gram)
    inv = jax.scipy.linalg.solve_triangular(lower, jnp.eye(rank, dtype=F32), lower=True)
    low, high = r_local[:half], r_local[half:]
    keep = jnp.where(core == 0, low, high) + other_core(jnp.where(core == 0, high, low))
    r_part = lax.all_to_all(keep.reshape(nz, half // nz, feat), "z", 0, 0, tiled=True)
    r_part, inv = tie((r_part, inv), three + [(3, 1), (3, 3)], True)
    r_part = jnp.sum(r_part, axis=0)
    four = fetch(((-1, 1), "x", 1), ((1, 2), "y", 1), ((-1, -1), "y", -1))
    use(three)
    r_part = jnp.sum(spread(r_part, MP), axis=0) / groups
    mine = tie(spread(r_part, "z"), four, True).reshape(half, feat)
    use(four)
    theirs = other_core(mine)
    r_all = jnp.concatenate([jnp.where(core == 0, mine, theirs), jnp.where(core == 0, theirs, mine)], axis=0)

    q_t = jnp.dot(inv, r_all, precision=hi)
    phat = jnp.dot(inv, pbar, precision=hi)

    mat, pre_grad = state
    ph, pw = split(phat, 2)
    qh, ql = split(q_t, 2)
    left = jnp.concatenate([ph, ph, pw], axis=0).T
    right = jnp.concatenate([qh, ql, qh], axis=0)
    new_error = new_errors(mat, error[:, None], left, right).transpose(1, 0, 2)
    return (pre_grad, new_error, q_t.T)


def solution(mesh):
    sizes = (mesh.shape["replica"] // 2, 2, 4, mesh.shape["mp"] // 4)
    grid = Mesh(mesh.devices.reshape(sizes), ALL)

    def run(*args):
        return shards(sizes, *args)

    return jax.shard_map(
        run,
        mesh=grid,
        in_specs=(
            P(MP, ("z", "core")),
            P(ALL, None),
            P(MP, None),
            P(("z", "core"), MP, None),
            P(),
        ),
        out_specs=(P(MP, ("z", "core")), P(("z", "core"), MP, None), P()),
        check_vma=False,
    )
```

```python
import functools

import jax
import jax.numpy as jnp
from jax import lax
from jax.experimental import pallas as pl
from jax.experimental.pallas import tpu as pltpu
from jax.sharding import Mesh, PartitionSpec as P

F32 = jnp.float32
BF16 = jnp.bfloat16
MP = ("y", "x")
ALL = ("z", "core", "y", "x")


def gelu_back(pre, grad):
    _, pull = jax.vjp(jax.nn.gelu, pre)
    return pull(grad)[0]


def gelu16(pre):
    return jax.nn.gelu(pre.astype(F32)).astype(BF16)


def split(x, parts):
    out = []
    for _ in range(parts):
        top = lax.reduce_precision(x, 8, 7)
        out.append(top.astype(BF16))
        x = x - top
    return out


def dot(a, b, ca, cb):
    return lax.dot_general(a, b, (((ca,), (cb,)), ((), ())), preferred_element_type=F32)


def fold(x, parts, axis=0):
    n = x.shape[axis] // parts
    return sum(lax.slice_in_dim(x, i * n, (i + 1) * n, axis=axis) for i in range(parts))


def spread(x, axis):
    n = lax.axis_size(axis)
    return lax.all_to_all(jnp.broadcast_to(x, (n,) + x.shape), axis, 0, 0, tiled=True)


def other_core(x):
    return lax.ppermute(x, "core", [(0, 1), (1, 0)])


def shift(x, axis, step):
    n = lax.axis_size(axis)
    return lax.ppermute(x, axis, [((i + step) % n, i) for i in range(n)])


def products(n, where, pre_ref, weight_ref, *refs):
    blocks, held, (mat_ref, grad_ref, pre_buf, weight_buf, sems) = refs[:n], refs[n:-5], refs[-5:]
    fetch_pre = pltpu.make_async_copy(pre_ref, pre_buf, sems.at[0])
    fetch_weight = pltpu.make_async_copy(weight_ref, weight_buf, sems.at[1])
    fetch_pre.start()
    fetch_weight.start()
    if held:
        grad_ref[...] = held[1][...]
    own = blocks[0].shape[1]
    spots = [pl.ds(pl.multiple_of(where[i] * own, own), own) for i in range(n)]
    fetch_pre.wait()
    pre = jnp.concatenate([pre_buf[:, s] for s in spots], axis=1).astype(F32)
    act, pull = jax.vjp(jax.nn.gelu, pre)
    act = act.astype(BF16)
    fetch_weight.wait()
    feat = weight_buf.shape[1]
    back = jnp.zeros(pre.shape, F32)
    for lo in range(0, feat, 512):
        part = slice(lo, min(feat, lo + 512))
        piece = jnp.concatenate([b[part, :] for b in blocks], axis=1)
        back = back + dot(weight_buf[:, part], piece, 1, 0)
        more = dot(act, piece, 1, 1)
        mat_ref[:, part] = more + held[0][:, part] if held else more
    out = pull(back)[0].astype(BF16)
    for i, s in enumerate(spots):
        grad_ref[:, s] = out[:, i * own:(i + 1) * own]


def add_products(where, pre_act, weight, blocks, held):
    vmem = pl.BlockSpec(memory_space=pltpu.VMEM)
    n = len(blocks)
    mat = jax.ShapeDtypeStruct(weight.shape, F32)
    return pl.pallas_call(
        functools.partial(products, n),
        out_shape=(mat, jax.ShapeDtypeStruct(pre_act.shape, BF16)),
        in_specs=[pl.BlockSpec(memory_space=pltpu.SMEM)]
        + [pl.BlockSpec(memory_space=pltpu.HBM)] * 2
        + [vmem] * (n + len(held)),
        out_specs=(vmem, vmem),
        scratch_shapes=[
            pltpu.VMEM(pre_act.shape, BF16),
            pltpu.VMEM(weight.shape, BF16),
            pltpu.SemaphoreType.DMA((2,)),
        ],
        input_output_aliases={n + 3: 0, n + 4: 1} if held else {},
        compiler_params=pltpu.CompilerParams(vmem_limit_bytes=12 * 2**20),
    )(where, pre_act, weight, *blocks, *held)


def finish(mat_ref, error_ref, left_ref, right_ref, out_ref):
    feat = mat_ref.shape[1]
    left = left_ref[...]
    for lo in range(0, feat, 512):
        part = slice(lo, min(feat, lo + 512))
        out_ref[:, 0, part] = mat_ref[:, part] + error_ref[:, 0, part] - dot(left, right_ref[:, part], 1, 0)


def new_errors(mat, error, left, right):
    vmem = pl.BlockSpec(memory_space=pltpu.VMEM)
    return pl.pallas_call(
        finish,
        out_shape=jax.ShapeDtypeStruct(error.shape, F32),
        in_specs=[vmem] * 4,
        out_specs=vmem,
        compiler_params=pltpu.CompilerParams(vmem_limit_bytes=12 * 2**20),
    )(mat, error, left, right)


def right_rows(z_ref, og_ref, more_ref, out_ref):
    rank, feat = out_ref.shape
    z = z_ref[...]
    for lo in range(0, feat, 512):
        part = slice(lo, min(feat, lo + 512))
        out_ref[:, part] = fold(dot(z, og_ref[part, :], 1, 1), 2) + more_ref[:, part]


def right_factor(z2, og, more):
    vmem = pl.BlockSpec(memory_space=pltpu.VMEM)
    return pl.pallas_call(
        right_rows,
        out_shape=jax.ShapeDtypeStruct(more.shape, F32),
        in_specs=[vmem] * 3,
        out_specs=vmem,
        compiler_params=pltpu.CompilerParams(vmem_limit_bytes=12 * 2**20),
    )(z2, og, more)


def shards(sizes, pre_act, out_grad, weight, error, q_init):
    hi = lax.Precision.HIGHEST
    nz, nc, ny, nx = sizes
    groups = nz * nc
    mp = ny * nx
    rank = q_init.shape[1]
    half = rank // 2
    hid, toks = pre_act.shape
    own, feat = out_grad.shape
    error = error[0]
    core = lax.axis_index("core")

    og = out_grad.T
    got = {(0, 0): og}
    iy, ix = lax.axis_index("y"), lax.axis_index("x")
    state = []

    def fetch(*moves):
        new = {}
        for key, axis, step in moves:
            dy, dx = (key[0] + step, key[1]) if axis == "y" else (key[0], key[1] + step)
            new[dy % ny, dx % nx] = shift(got[key[0] % ny, key[1] % nx], axis, step)
        got.update(new)
        return list(new)

    def tie(value, keys=(), with_state=False):
        out = lax.optimization_barrier([value, [got[k] for k in keys], state if with_state else []])
        got.update(zip(keys, out[1]))
        if with_state:
            state[:] = out[2]
        return out[0]

    def use(keys):
        where = jnp.stack([((iy + dy) & (ny - 1)) * nx + ((ix + dx) & (nx - 1)) for dy, dx in keys])
        state[:] = add_products(where, pre_act, weight, [got[k] for k in keys], state)

    one = fetch(((0, 0), "x", 1), ((0, 0), "x", -1), ((0, 0), "y", 1), ((0, 0), "y", -1))

    act = gelu16(pre_act)
    q2 = jnp.concatenate(split(q_init, 2), axis=1)
    y = fold(dot(q2, out_grad, 0, 1), 2)
    y_all = tie(spread(y, MP), one)
    two = fetch(((0, 1), "y", 1), ((0, -1), "y", -1), ((1, 0), "x", -1), ((-1, 0), "x", 1))
    use([(0, 0)] + one)
    y_all = y_all.transpose(1, 0, 2).reshape(rank, toks)
    y2 = jnp.concatenate(split(y_all, 2), axis=0)
    e2 = split(error, 2)
    p_err = sum(fold(dot(q2, e, 0, 1), 2) for e in e2)
    p_local = fold(dot(y2, act, 1, 1), 2) + p_err
    pbar = jnp.sum(tie(spread(p_local, "z"), [], True), axis=0)
    pbar = tie((pbar + other_core(pbar)) / groups, two)

    l2 = jnp.concatenate(split(pbar, 2), axis=0)
    r_error = fold(dot(l2, e2[0], 1, 0), 2)
    z_part = fold(dot(l2, act, 1, 0), 2)
    gram_part = jnp.dot(pbar, pbar.T, precision=hi)
    side = 128 // rank
    flat = jnp.concatenate(jnp.split(gram_part, side, axis=0), axis=1)
    sent = jnp.concatenate(
        [
            z_part.reshape(rank, mp, own).transpose(1, 0, 2),
            jnp.broadcast_to(flat, (mp,) + flat.shape),
        ],
        axis=1,
    )
    took = tie(lax.all_to_all(sent, MP, 0, 0, tiled=True), two + [(0, 1), (1, 0)])
    three = fetch(((0, 1), "x", 1), ((1, 0), "y", 1), ((1, -1), "x", -1), ((-1, 1), "y", -1))
    use(two)
    took = jnp.sum(took, axis=0)
    z = took[:rank]
    gram = jnp.concatenate(jnp.split(took[rank:], side, axis=1), axis=0)

    z2 = jnp.concatenate(split(z, 2), axis=0)
    r_local = right_factor(z2, og, r_error)
    low, high = r_local[:half], r_local[half:]
    keep = jnp.where(core == 0, low, high) + other_core(jnp.where(core == 0, high, low))
    r_part = lax.all_to_all(keep.reshape(nz, half // nz, feat), "z", 0, 0, tiled=True)
    r_part = jnp.sum(tie(r_part, three + [(3, 1), (3, 3)], True), axis=0)
    four = fetch(((-1, 1), "x", 1), ((1, 2), "y", 1), ((-1, -1), "y", -1))
    use(three)
    r_part, gram = tie((spread(r_part, MP), gram))
    r_part = jnp.sum(r_part, axis=0) / groups
    lower = jnp.linalg.cholesky(gram)
    inv = jax.scipy.linalg.solve_triangular(lower, jnp.eye(rank, dtype=F32), lower=True)
    mine = tie(spread(r_part, "z"), four, True).reshape(half, feat)
    use(four)
    theirs = other_core(mine)
    r_all = jnp.concatenate([jnp.where(core == 0, mine, theirs), jnp.where(core == 0, theirs, mine)], axis=0)

    q_t = jnp.dot(inv, r_all, precision=hi)
    phat = jnp.dot(inv, pbar, precision=hi)

    mat, pre_grad = state
    ph, pw = split(phat, 2)
    qh, ql = split(q_t, 2)
    left = jnp.concatenate([ph, ph, pw], axis=0).T
    right = jnp.concatenate([qh, ql, qh], axis=0)
    new_error = new_errors(mat, error[:, None], left, right).transpose(1, 0, 2)
    return (pre_grad, new_error, q_t.T)


def solution(mesh):
    sizes = (mesh.shape["replica"] // 2, 2, 4, mesh.shape["mp"] // 4)
    grid = Mesh(mesh.devices.reshape(sizes), ALL)

    def run(*args):
        return shards(sizes, *args)

    return jax.shard_map(
        run,
        mesh=grid,
        in_specs=(
            P(MP, ("z", "core")),
            P(ALL, None),
            P(MP, None),
            P(("z", "core"), MP, None),
            P(),
        ),
        out_specs=(P(MP, ("z", "core")), P(("z", "core"), MP, None), P()),
        check_vma=False,
    )
```

```python
import functools

import jax
import jax.numpy as jnp
from jax import lax
from jax.experimental import pallas as pl
from jax.experimental.pallas import tpu as pltpu
from jax.sharding import Mesh, PartitionSpec as P

F32 = jnp.float32
BF16 = jnp.bfloat16
MP = ("y", "x")
ALL = ("z", "core", "y", "x")


def gelu_back(pre, grad):
    _, pull = jax.vjp(jax.nn.gelu, pre)
    return pull(grad)[0]


def gelu16(pre):
    return jax.nn.gelu(pre.astype(F32)).astype(BF16)


def split(x, parts):
    out = []
    for _ in range(parts):
        top = lax.reduce_precision(x, 8, 7)
        out.append(top.astype(BF16))
        x = x - top
    return out


def dot(a, b, ca, cb):
    return lax.dot_general(a, b, (((ca,), (cb,)), ((), ())), preferred_element_type=F32)


def fold(x, parts, axis=0):
    n = x.shape[axis] // parts
    return sum(lax.slice_in_dim(x, i * n, (i + 1) * n, axis=axis) for i in range(parts))


def spread(x, axis):
    n = lax.axis_size(axis)
    return lax.all_to_all(jnp.broadcast_to(x, (n,) + x.shape), axis, 0, 0, tiled=True)


def other_core(x):
    return lax.ppermute(x, "core", [(0, 1), (1, 0)])


def shift(x, axis, step):
    n = lax.axis_size(axis)
    return lax.ppermute(x, axis, [((i + step) % n, i) for i in range(n)])


def products(n, last, where, pre_ref, weight_ref, *refs):
    blocks, refs = refs[:n], refs[n:]
    held, (mat_ref, grad_ref) = refs[:-2], refs[-2:]
    if held:
        grad_ref[...] = held[1][...]
    rows = grad_ref.shape[0]
    own = blocks[0].shape[1]
    spots = [pl.ds(pl.multiple_of(where[i] * own, own), own) for i in range(n)]
    pre = jnp.concatenate([pre_ref[:, s] for s in spots], axis=1).astype(F32)
    act, pull = jax.vjp(jax.nn.gelu, pre)
    act = act.astype(BF16)
    feat = weight_ref.shape[1]
    back = jnp.zeros(pre.shape, F32)
    for lo in range(0, feat, 512):
        part = slice(lo, min(feat, lo + 512))
        piece = jnp.concatenate([b[part, :] for b in blocks], axis=1)
        back = back + dot(weight_ref[:, part], piece, 1, 0)
        more = dot(act, piece, 1, 1)
        if held:
            more = more + held[0][:, part]
        if last:
            error_ref, left_ref, right_ref = held[2:]
            low_rank = dot(left_ref[...], right_ref[:, part], 1, 0)
            mat_ref[:, 0, part] = more[:rows] + error_ref[:, 0, part] - low_rank
        else:
            mat_ref[:, part] = more
    out = pull(back)[0].astype(BF16)
    for i, s in enumerate(spots):
        grad_ref[:, s] = out[:rows, i * own:(i + 1) * own]


def add_products(where, rows, pre, weight, blocks, held, finish=()):
    vmem = pl.BlockSpec(memory_space=pltpu.VMEM)
    n = len(blocks)
    mat = (rows, 1, weight.shape[1]) if finish else weight.shape
    aliases = {n + 4: 1} if held else {}
    if held and not finish:
        aliases[n + 3] = 0
    return pl.pallas_call(
        functools.partial(products, n, bool(finish)),
        out_shape=(jax.ShapeDtypeStruct(mat, F32), jax.ShapeDtypeStruct((rows, pre.shape[1]), BF16)),
        in_specs=[pl.BlockSpec(memory_space=pltpu.SMEM)] + [vmem] * (n + 2 + len(held) + len(finish)),
        out_specs=(vmem, vmem),
        input_output_aliases=aliases,
        compiler_params=pltpu.CompilerParams(vmem_limit_bytes=14 * 2**20),
    )(where, pre, weight, *blocks, *held, *finish)


def right_rows(z_ref, og_ref, more_ref, out_ref):
    rank, feat = out_ref.shape
    z = z_ref[...]
    for lo in range(0, feat, 512):
        part = slice(lo, min(feat, lo + 512))
        out_ref[:, part] = fold(dot(z, og_ref[part, :], 1, 1), 2) + more_ref[:, part]


def right_factor(z2, og, more):
    vmem = pl.BlockSpec(memory_space=pltpu.VMEM)
    return pl.pallas_call(
        right_rows,
        out_shape=jax.ShapeDtypeStruct(more.shape, F32),
        in_specs=[vmem] * 3,
        out_specs=vmem,
        compiler_params=pltpu.CompilerParams(vmem_limit_bytes=12 * 2**20),
    )(z2, og, more)


def shards(sizes, pre_act, out_grad, weight, error, q_init):
    hi = lax.Precision.HIGHEST
    nz, nc, ny, nx = sizes
    groups = nz * nc
    mp = ny * nx
    rank = q_init.shape[1]
    half = rank // 2
    hid, toks = pre_act.shape
    own, feat = out_grad.shape
    error = error[0]
    core = lax.axis_index("core")

    og = out_grad.T
    got = {(0, 0): og}
    iy, ix = lax.axis_index("y"), lax.axis_index("x")
    state = []

    def fetch(*moves):
        new = {}
        for key, axis, step in moves:
            dy, dx = (key[0] + step, key[1]) if axis == "y" else (key[0], key[1] + step)
            new[dy % ny, dx % nx] = shift(got[key[0] % ny, key[1] % nx], axis, step)
        got.update(new)
        return list(new)

    def tie(value, keys=(), with_state=False):
        out = lax.optimization_barrier([value, [got[k] for k in keys], state if with_state else []])
        got.update(zip(keys, out[1]))
        if with_state:
            state[:] = out[2]
        return out[0]

    pad = ((0, -hid % 16), (0, 0))
    pre_pad, w_pad = jnp.pad(pre_act, pad), jnp.pad(weight, pad)

    def use(keys, finish=()):
        where = jnp.stack([((iy + dy) & (ny - 1)) * nx + ((ix + dx) & (nx - 1)) for dy, dx in keys])
        state[:] = add_products(where, hid, pre_pad, w_pad, [got[k] for k in keys], state, finish)

    one = fetch(((0, 0), "x", 1), ((0, 0), "x", -1), ((0, 0), "y", 1), ((0, 0), "y", -1))

    act = gelu16(pre_act)
    q2 = jnp.concatenate(split(q_init, 2), axis=1)
    y = fold(dot(q2, out_grad, 0, 1), 2)
    y_all = tie(spread(y, MP), one)
    two = fetch(((0, 1), "y", 1), ((0, -1), "y", -1), ((1, 0), "x", -1), ((-1, 0), "x", 1))
    use([(0, 0)] + one)
    y_all = y_all.transpose(1, 0, 2).reshape(rank, toks)
    y2 = jnp.concatenate(split(y_all, 2), axis=0)
    e2 = split(error, 2)
    p_err = sum(fold(dot(q2, e, 0, 1), 2) for e in e2)
    p_local = fold(dot(y2, act, 1, 1), 2) + p_err
    pbar = jnp.sum(tie(spread(p_local, "z"), [], True), axis=0)
    pbar = tie((pbar + other_core(pbar)) / groups, two)

    l2 = jnp.concatenate(split(pbar, 2), axis=0)
    r_error = fold(dot(l2, e2[0], 1, 0), 2)
    z_part = fold(dot(l2, act, 1, 0), 2)
    gram_part = jnp.dot(pbar, pbar.T, precision=hi)
    side = 128 // rank
    flat = jnp.concatenate(jnp.split(gram_part, side, axis=0), axis=1)
    sent = jnp.concatenate(
        [
            z_part.reshape(rank, mp, own).transpose(1, 0, 2),
            jnp.broadcast_to(flat, (mp,) + flat.shape),
        ],
        axis=1,
    )
    took = tie(lax.all_to_all(sent, MP, 0, 0, tiled=True), two + [(0, 1), (1, 0)])
    three = fetch(((0, 1), "x", 1), ((1, 0), "y", 1), ((1, -1), "x", -1), ((-1, 1), "y", -1))
    took = jnp.sum(took, axis=0)
    z = took[:rank]
    gram = jnp.concatenate(jnp.split(took[rank:], side, axis=1), axis=0)

    z2 = jnp.concatenate(split(z, 2), axis=0)
    r_local = right_factor(z2, og, r_error)
    low, high = r_local[:half], r_local[half:]
    keep = jnp.where(core == 0, low, high) + other_core(jnp.where(core == 0, high, low))
    keep = tie(keep, two, True)
    use(two)
    gram = tie(gram, [], True)
    lower = jnp.linalg.cholesky(gram)
    inv = jax.scipy.linalg.solve_triangular(lower, jnp.eye(rank, dtype=F32), lower=True)
    r_part = lax.all_to_all(keep.reshape(nz, half // nz, feat), "z", 0, 0, tiled=True)
    r_part, inv = tie((r_part, inv), three + [(3, 1), (3, 3)], True)
    r_part = jnp.sum(r_part, axis=0)
    four = fetch(((-1, 1), "x", 1), ((1, 2), "y", 1), ((-1, -1), "y", -1))
    r_part = tie(spread(r_part, MP), [], True)
    use(three)
    r_part = jnp.sum(r_part, axis=0) / groups
    mine = tie(spread(r_part, "z"), four, True).reshape(half, feat)
    theirs = other_core(mine)
    r_all = jnp.concatenate([jnp.where(core == 0, mine, theirs), jnp.where(core == 0, theirs, mine)], axis=0)

    q_t = jnp.dot(inv, r_all, precision=hi)
    phat = jnp.dot(inv, pbar, precision=hi)

    ph, pw = split(phat, 2)
    qh, ql = split(q_t, 2)
    left = jnp.concatenate([ph, ph, pw], axis=0).T
    right = jnp.concatenate([qh, ql, qh], axis=0)
    use(four, (error[:, None], left, right))
    new_error, pre_grad = state
    new_error = new_error.transpose(1, 0, 2)
    return (pre_grad, new_error, q_t.T)


def solution(mesh):
    sizes = (mesh.shape["replica"] // 2, 2, 4, mesh.shape["mp"] // 4)
    grid = Mesh(mesh.devices.reshape(sizes), ALL)

    def run(*args):
        return shards(sizes, *args)

    return jax.shard_map(
        run,
        mesh=grid,
        in_specs=(
            P(MP, ("z", "core")),
            P(ALL, None),
            P(MP, None),
            P(("z", "core"), MP, None),
            P(),
        ),
        out_specs=(P(MP, ("z", "core")), P(("z", "core"), MP, None), P()),
        check_vma=False,
    )
```

```python
import functools

import jax
import jax.numpy as jnp
from jax import lax
from jax.experimental import pallas as pl
from jax.experimental.pallas import tpu as pltpu
from jax.sharding import Mesh, PartitionSpec as P

F32 = jnp.float32
BF16 = jnp.bfloat16
MP = ("y", "x")
ALL = ("z", "core", "y", "x")


def gelu_back(pre, grad):
    _, pull = jax.vjp(jax.nn.gelu, pre)
    return pull(grad)[0]


def gelu16(pre):
    return jax.nn.gelu(pre.astype(F32)).astype(BF16)


def split(x, parts):
    out = []
    for _ in range(parts):
        top = lax.reduce_precision(x, 8, 7)
        out.append(top.astype(BF16))
        x = x - top
    return out


def dot(a, b, ca, cb):
    return lax.dot_general(a, b, (((ca,), (cb,)), ((), ())), preferred_element_type=F32)


def fold(x, parts, axis=0):
    n = x.shape[axis] // parts
    return sum(lax.slice_in_dim(x, i * n, (i + 1) * n, axis=axis) for i in range(parts))


def spread(x, axis):
    n = lax.axis_size(axis)
    return lax.all_to_all(jnp.broadcast_to(x, (n,) + x.shape), axis, 0, 0, tiled=True)


def other_core(x):
    return lax.ppermute(x, "core", [(0, 1), (1, 0)])


def shift(x, axis, step):
    n = lax.axis_size(axis)
    return lax.ppermute(x, axis, [((i + step) % n, i) for i in range(n)])


def products(n, where, pre_ref, weight_ref, *refs):
    blocks, held, (mat_ref, grad_ref) = refs[:n], refs[n:-2], refs[-2:]
    if held:
        grad_ref[...] = held[1][...]
    rows = grad_ref.shape[0]
    own = blocks[0].shape[1]
    spots = [pl.ds(pl.multiple_of(where[i] * own, own), own) for i in range(n)]
    pre = jnp.concatenate([pre_ref[:, s] for s in spots], axis=1).astype(F32)
    act, pull = jax.vjp(jax.nn.gelu, pre)
    act = act.astype(BF16)
    feat = weight_ref.shape[1]
    back = jnp.zeros(pre.shape, F32)
    for lo in range(0, feat, 512):
        part = slice(lo, min(feat, lo + 512))
        piece = jnp.concatenate([b[part, :] for b in blocks], axis=1)
        back = back + dot(weight_ref[:, part], piece, 1, 0)
        more = dot(act, piece, 1, 1)
        mat_ref[:, part] = more + held[0][:, part] if held else more
    out = pull(back)[0].astype(BF16)
    for i, s in enumerate(spots):
        grad_ref[:, s] = out[:rows, i * own:(i + 1) * own]


def add_products(where, rows, pre, weight, blocks, held):
    vmem = pl.BlockSpec(memory_space=pltpu.VMEM)
    n = len(blocks)
    mat = jax.ShapeDtypeStruct(weight.shape, F32)
    return pl.pallas_call(
        functools.partial(products, n),
        out_shape=(mat, jax.ShapeDtypeStruct((rows, pre.shape[1]), BF16)),
        in_specs=[pl.BlockSpec(memory_space=pltpu.SMEM)] + [vmem] * (n + 2 + len(held)),
        out_specs=(vmem, vmem),
        input_output_aliases={n + 3: 0, n + 4: 1} if held else {},
        compiler_params=pltpu.CompilerParams(vmem_limit_bytes=9 * 2**20),
    )(where, pre, weight, *blocks, *held)


def finish(mat_ref, error_ref, left_ref, right_ref, out_ref):
    rows, _, feat = error_ref.shape
    left = left_ref[...]
    for lo in range(0, feat, 512):
        part = slice(lo, min(feat, lo + 512))
        low_rank = dot(left, right_ref[:, part], 1, 0)
        out_ref[:, 0, part] = mat_ref[:, part][:rows] + error_ref[:, 0, part] - low_rank


def new_errors(mat, error, left, right):
    vmem = pl.BlockSpec(memory_space=pltpu.VMEM)
    return pl.pallas_call(
        finish,
        out_shape=jax.ShapeDtypeStruct(error.shape, F32),
        in_specs=[vmem] * 4,
        out_specs=vmem,
        compiler_params=pltpu.CompilerParams(vmem_limit_bytes=12 * 2**20),
    )(mat, error, left, right)


def right_rows(z_ref, og_ref, more_ref, out_ref):
    rank, feat = out_ref.shape
    z = z_ref[...]
    for lo in range(0, feat, 512):
        part = slice(lo, min(feat, lo + 512))
        out_ref[:, part] = fold(dot(z, og_ref[part, :], 1, 1), 2) + more_ref[:, part]


def right_factor(z2, og, more):
    vmem = pl.BlockSpec(memory_space=pltpu.VMEM)
    return pl.pallas_call(
        right_rows,
        out_shape=jax.ShapeDtypeStruct(more.shape, F32),
        in_specs=[vmem] * 3,
        out_specs=vmem,
        compiler_params=pltpu.CompilerParams(vmem_limit_bytes=8 * 2**20),
    )(z2, og, more)


def shards(sizes, pre_act, out_grad, weight, error, q_init):
    hi = lax.Precision.HIGHEST
    nz, nc, ny, nx = sizes
    groups = nz * nc
    mp = ny * nx
    rank = q_init.shape[1]
    half = rank // 2
    hid, toks = pre_act.shape
    own, feat = out_grad.shape
    error = error[0]
    core = lax.axis_index("core")

    og = out_grad.T
    got = {(0, 0): og}
    iy, ix = lax.axis_index("y"), lax.axis_index("x")
    state = []

    def fetch(*moves):
        new = {}
        for key, axis, step in moves:
            dy, dx = (key[0] + step, key[1]) if axis == "y" else (key[0], key[1] + step)
            new[dy % ny, dx % nx] = shift(got[key[0] % ny, key[1] % nx], axis, step)
        got.update(new)
        return list(new)

    def tie(value, keys=(), with_state=False):
        out = lax.optimization_barrier([value, [got[k] for k in keys], state if with_state else []])
        got.update(zip(keys, out[1]))
        if with_state:
            state[:] = out[2]
        return out[0]

    pad = ((0, -hid % 16), (0, 0))
    pre_pad, w_pad = jnp.pad(pre_act, pad), jnp.pad(weight, pad)

    def use(keys):
        where = jnp.stack([((iy + dy) & (ny - 1)) * nx + ((ix + dx) & (nx - 1)) for dy, dx in keys])
        state[:] = add_products(where, hid, pre_pad, w_pad, [got[k] for k in keys], state)

    one = fetch(((0, 0), "x", 1), ((0, 0), "x", -1), ((0, 0), "y", 1), ((0, 0), "y", -1))

    act = gelu16(pre_act)
    q2 = jnp.concatenate(split(q_init, 2), axis=1)
    y = fold(dot(q2, out_grad, 0, 1), 2)
    y_all = tie(spread(y, MP), one)
    two = fetch(((0, 1), "y", 1), ((0, -1), "y", -1), ((1, 0), "x", -1), ((-1, 0), "x", 1))
    use([(0, 0)] + one)
    y_all = y_all.transpose(1, 0, 2).reshape(rank, toks)
    y2 = jnp.concatenate(split(y_all, 2), axis=0)
    e2 = split(error, 2)
    p_err = sum(fold(dot(q2, e, 0, 1), 2) for e in e2)
    p_local = fold(dot(y2, act, 1, 1), 2) + p_err
    pbar = jnp.sum(tie(spread(p_local, "z"), [], True), axis=0)
    pbar = tie((pbar + other_core(pbar)) / groups, two)

    l2 = jnp.concatenate(split(pbar, 2), axis=0)
    r_error = fold(dot(l2, e2[0], 1, 0), 2)
    z_part = fold(dot(l2, act, 1, 0), 2)
    gram_part = jnp.dot(pbar, pbar.T, precision=hi)
    side = 128 // rank
    flat = jnp.concatenate(jnp.split(gram_part, side, axis=0), axis=1)
    sent = jnp.concatenate(
        [
            z_part.reshape(rank, mp, own).transpose(1, 0, 2),
            jnp.broadcast_to(flat, (mp,) + flat.shape),
        ],
        axis=1,
    )
    took = tie(lax.all_to_all(sent, MP, 0, 0, tiled=True), two + [(0, 1), (1, 0)])
    three = fetch(((0, 1), "x", 1), ((1, 0), "y", 1), ((1, -1), "x", -1), ((-1, 1), "y", -1))
    use(two)
    took = jnp.sum(took, axis=0)
    z = took[:rank]
    gram = jnp.concatenate(jnp.split(took[rank:], side, axis=1), axis=0)

    z2 = jnp.concatenate(split(z, 2), axis=0)
    r_local = right_factor(z2, og, r_error)
    low, high = r_local[:half], r_local[half:]
    keep = jnp.where(core == 0, low, high) + other_core(jnp.where(core == 0, high, low))
    r_part = lax.all_to_all(keep.reshape(nz, half // nz, feat), "z", 0, 0, tiled=True)
    r_part = jnp.sum(tie(r_part, three + [(3, 1), (3, 3)], True), axis=0)
    four = fetch(((-1, 1), "x", 1), ((1, 2), "y", 1), ((-1, -1), "y", -1))
    use(three)
    r_part, gram = tie((spread(r_part, MP), gram))
    r_part = jnp.sum(r_part, axis=0) / groups
    lower = jnp.linalg.cholesky(gram)
    inv = jax.scipy.linalg.solve_triangular(lower, jnp.eye(rank, dtype=F32), lower=True)
    mine = tie(spread(r_part, "z"), four, True).reshape(half, feat)
    use(four)
    theirs = other_core(mine)
    r_all = jnp.concatenate([jnp.where(core == 0, mine, theirs), jnp.where(core == 0, theirs, mine)], axis=0)

    q_t = jnp.dot(inv, r_all, precision=hi)
    phat = jnp.dot(inv, pbar, precision=hi)

    ph, pw = split(phat, 2)
    qh, ql = split(q_t, 2)
    left = jnp.concatenate([ph, ph, pw], axis=0).T
    right = jnp.concatenate([qh, ql, qh], axis=0)
    mat, pre_grad = state
    new_error = new_errors(mat, error[:, None], left, right).transpose(1, 0, 2)
    return (pre_grad, new_error, q_t.T)


def solution(mesh):
    sizes = (mesh.shape["replica"] // 2, 2, 4, mesh.shape["mp"] // 4)
    grid = Mesh(mesh.devices.reshape(sizes), ALL)

    def run(*args):
        return shards(sizes, *args)

    return jax.shard_map(
        run,
        mesh=grid,
        in_specs=(
            P(MP, ("z", "core")),
            P(ALL, None),
            P(MP, None),
            P(("z", "core"), MP, None),
            P(),
        ),
        out_specs=(P(MP, ("z", "core")), P(("z", "core"), MP, None), P()),
        check_vma=False,
    )
```

```python
import functools

import jax
import jax.numpy as jnp
from jax import lax
from jax.experimental import pallas as pl
from jax.experimental.pallas import tpu as pltpu
from jax.sharding import Mesh, PartitionSpec as P

F32 = jnp.float32
BF16 = jnp.bfloat16
MP = ("y", "x")
ALL = ("z", "core", "y", "x")


def gelu_back(pre, grad):
    _, pull = jax.vjp(jax.nn.gelu, pre)
    return pull(grad)[0]


def gelu16(pre):
    return jax.nn.gelu(pre.astype(F32)).astype(BF16)


def split(x, parts):
    out = []
    for _ in range(parts):
        top = lax.reduce_precision(x, 8, 7)
        out.append(top.astype(BF16))
        x = x - top
    return out


def dot(a, b, ca, cb):
    return lax.dot_general(a, b, (((ca,), (cb,)), ((), ())), preferred_element_type=F32)


def fold(x, parts, axis=0):
    n = x.shape[axis] // parts
    return sum(lax.slice_in_dim(x, i * n, (i + 1) * n, axis=axis) for i in range(parts))


def spread(x, axis):
    n = lax.axis_size(axis)
    return lax.all_to_all(jnp.broadcast_to(x, (n,) + x.shape), axis, 0, 0, tiled=True)


def other_core(x):
    return lax.ppermute(x, "core", [(0, 1), (1, 0)])


def shift(x, axis, step):
    n = lax.axis_size(axis)
    return lax.ppermute(x, axis, [((i + step) % n, i) for i in range(n)])


def products(n, where, pre_ref, weight_ref, *refs):
    blocks, held, (mat_ref, grad_ref) = refs[:n], refs[n:-2], refs[-2:]
    if held:
        grad_ref[...] = held[1][...]
    rows = grad_ref.shape[0]
    own = blocks[0].shape[1]
    spots = [pl.ds(pl.multiple_of(where[i] * own, own), own) for i in range(n)]
    pre = jnp.concatenate([pre_ref[:, s] for s in spots], axis=1).astype(F32)
    act, pull = jax.vjp(jax.nn.gelu, pre)
    act = act.astype(BF16)
    feat = weight_ref.shape[1]
    back = jnp.zeros(pre.shape, F32)
    for lo in range(0, feat, 512):
        part = slice(lo, min(feat, lo + 512))
        piece = jnp.concatenate([b[part, :] for b in blocks], axis=1)
        back = back + dot(weight_ref[:, part], piece, 1, 0)
        more = dot(act, piece, 1, 1)
        mat_ref[:, part] = more + held[0][:, part] if held else more
    out = pull(back)[0].astype(BF16)
    for i, s in enumerate(spots):
        grad_ref[:, s] = out[:rows, i * own:(i + 1) * own]


def add_products(where, rows, pre, weight, blocks, held):
    vmem = pl.BlockSpec(memory_space=pltpu.VMEM)
    n = len(blocks)
    mat = jax.ShapeDtypeStruct(weight.shape, F32)
    return pl.pallas_call(
        functools.partial(products, n),
        out_shape=(mat, jax.ShapeDtypeStruct((rows, pre.shape[1]), BF16)),
        in_specs=[pl.BlockSpec(memory_space=pltpu.SMEM)] + [vmem] * (n + 2 + len(held)),
        out_specs=(vmem, vmem),
        input_output_aliases={n + 3: 0, n + 4: 1} if held else {},
        compiler_params=pltpu.CompilerParams(vmem_limit_bytes=12 * 2**20),
    )(where, pre, weight, *blocks, *held)


def finish(mat_ref, error_ref, left_ref, right_ref, out_ref):
    rows, _, feat = error_ref.shape
    left = left_ref[...]
    for lo in range(0, feat, 512):
        part = slice(lo, min(feat, lo + 512))
        low_rank = dot(left, right_ref[:, part], 1, 0)
        out_ref[:, 0, part] = mat_ref[:, part][:rows] + error_ref[:, 0, part] - low_rank


def new_errors(mat, error, left, right):
    vmem = pl.BlockSpec(memory_space=pltpu.VMEM)
    return pl.pallas_call(
        finish,
        out_shape=jax.ShapeDtypeStruct(error.shape, F32),
        in_specs=[vmem] * 4,
        out_specs=vmem,
        compiler_params=pltpu.CompilerParams(vmem_limit_bytes=12 * 2**20),
    )(mat, error, left, right)


def right_rows(z_ref, og_ref, more_ref, out_ref):
    rank, feat = out_ref.shape
    z = z_ref[...]
    for lo in range(0, feat, 512):
        part = slice(lo, min(feat, lo + 512))
        out_ref[:, part] = fold(dot(z, og_ref[part, :], 1, 1), 2) + more_ref[:, part]


def right_factor(z2, og, more):
    vmem = pl.BlockSpec(memory_space=pltpu.VMEM)
    return pl.pallas_call(
        right_rows,
        out_shape=jax.ShapeDtypeStruct(more.shape, F32),
        in_specs=[vmem] * 3,
        out_specs=vmem,
        compiler_params=pltpu.CompilerParams(vmem_limit_bytes=12 * 2**20),
    )(z2, og, more)


def shards(sizes, pre_act, out_grad, weight, error, q_init):
    hi = lax.Precision.HIGHEST
    nz, nc, ny, nx = sizes
    groups = nz * nc
    mp = ny * nx
    rank = q_init.shape[1]
    half = rank // 2
    hid, toks = pre_act.shape
    own, feat = out_grad.shape
    error = error[0]
    core = lax.axis_index("core")

    og = out_grad.T
    got = {(0, 0): og}
    iy, ix = lax.axis_index("y"), lax.axis_index("x")
    state = []

    def fetch(*moves):
        new = {}
        for key, axis, step in moves:
            dy, dx = (key[0] + step, key[1]) if axis == "y" else (key[0], key[1] + step)
            new[dy % ny, dx % nx] = shift(got[key[0] % ny, key[1] % nx], axis, step)
        got.update(new)
        return list(new)

    def tie(value, keys=(), with_state=False):
        out = lax.optimization_barrier([value, [got[k] for k in keys], state if with_state else []])
        got.update(zip(keys, out[1]))
        if with_state:
            state[:] = out[2]
        return out[0]

    def use(keys):
        where = jnp.stack([((iy + dy) & (ny - 1)) * nx + ((ix + dx) & (nx - 1)) for dy, dx in keys])
        state[:] = add_products(where, hid, pre_act, weight, [got[k] for k in keys], state)

    one = fetch(((0, 0), "x", 1), ((0, 0), "x", -1), ((0, 0), "y", 1), ((0, 0), "y", -1))

    act = gelu16(pre_act)
    q2 = jnp.concatenate(split(q_init, 2), axis=1)
    y = fold(dot(q2, out_grad, 0, 1), 2)
    y_all = tie(spread(y, MP), one)
    two = fetch(((0, 1), "y", 1), ((0, -1), "y", -1), ((1, 0), "x", -1), ((-1, 0), "x", 1))
    use([(0, 0)] + one)
    y_all = y_all.transpose(1, 0, 2).reshape(rank, toks)
    y2 = jnp.concatenate(split(y_all, 2), axis=0)
    e2 = split(error, 2)
    p_err = sum(fold(dot(q2, e, 0, 1), 2) for e in e2)
    p_local = fold(dot(y2, act, 1, 1), 2) + p_err
    pbar = jnp.sum(tie(spread(p_local, "z"), [], True), axis=0)
    pbar = tie((pbar + other_core(pbar)) / groups, two)

    l2 = jnp.concatenate(split(pbar, 2), axis=0)
    r_error = fold(dot(l2, e2[0], 1, 0), 2)
    z_part = fold(dot(l2, act, 1, 0), 2)
    gram_part = jnp.dot(pbar, pbar.T, precision=hi)
    side = 128 // rank
    flat = jnp.concatenate(jnp.split(gram_part, side, axis=0), axis=1)
    sent = jnp.concatenate(
        [
            z_part.reshape(rank, mp, own).transpose(1, 0, 2),
            jnp.broadcast_to(flat, (mp,) + flat.shape),
        ],
        axis=1,
    )
    took = tie(lax.all_to_all(sent, MP, 0, 0, tiled=True), two + [(0, 1), (1, 0)])
    three = fetch(((0, 1), "x", 1), ((1, 0), "y", 1), ((1, -1), "x", -1), ((-1, 1), "y", -1))
    use(two)
    took = jnp.sum(took, axis=0)
    z = took[:rank]
    gram = jnp.concatenate(jnp.split(took[rank:], side, axis=1), axis=0)

    z2 = jnp.concatenate(split(z, 2), axis=0)
    r_local = right_factor(z2, og, r_error)
    low, high = r_local[:half], r_local[half:]
    keep = jnp.where(core == 0, low, high) + other_core(jnp.where(core == 0, high, low))
    r_part = lax.all_to_all(keep.reshape(nz, half // nz, feat), "z", 0, 0, tiled=True)
    r_part = jnp.sum(tie(r_part, three + [(3, 1), (3, 3)], True), axis=0)
    four = fetch(((-1, 1), "x", 1), ((1, 2), "y", 1), ((-1, -1), "y", -1))
    use(three)
    r_part, gram = tie((spread(r_part, MP), gram))
    r_part = jnp.sum(r_part, axis=0) / groups
    lower = jnp.linalg.cholesky(gram)
    inv = jax.scipy.linalg.solve_triangular(lower, jnp.eye(rank, dtype=F32), lower=True)
    mine = tie(spread(r_part, "z"), four, True).reshape(half, feat)
    use(four)
    theirs = other_core(mine)
    r_all = jnp.concatenate([jnp.where(core == 0, mine, theirs), jnp.where(core == 0, theirs, mine)], axis=0)

    q_t = jnp.dot(inv, r_all, precision=hi)
    phat = jnp.dot(inv, pbar, precision=hi)

    ph, pw = split(phat, 2)
    qh, ql = split(q_t, 2)
    left = jnp.concatenate([ph, ph, pw], axis=0).T
    right = jnp.concatenate([qh, ql, qh], axis=0)
    mat, pre_grad = state
    new_error = new_errors(mat, error[:, None], left, right).transpose(1, 0, 2)
    return (pre_grad, new_error, q_t.T)


def solution(mesh):
    sizes = (mesh.shape["replica"] // 2, 2, 4, mesh.shape["mp"] // 4)
    grid = Mesh(mesh.devices.reshape(sizes), ALL)

    def run(*args):
        return shards(sizes, *args)

    return jax.shard_map(
        run,
        mesh=grid,
        in_specs=(
            P(MP, ("z", "core")),
            P(ALL, None),
            P(MP, None),
            P(("z", "core"), MP, None),
            P(),
        ),
        out_specs=(P(MP, ("z", "core")), P(("z", "core"), MP, None), P()),
        check_vma=False,
    )
```
